32 devices in a mesh: wide: 8 (over z, y), narrow: 4 (over x, core).
Axes of the slice: x: 2, y: 2, z: 4, core: 2. Of those that a mesh axis runs over, the one named last changes fastest.
Arguments:
- dense_feats: bfloat16 [32768, 384], P(('wide', 'narrow')), may hold values from -6 to 6
- sparse_ids: int32 [32768, 8], P(('wide', 'narrow')), may hold values from 0 to 1023
- presence: int32 [32768, 8], P(('wide', 'narrow')), may hold values 0 or 1
- embed_table: bfloat16 [1024, 16], replicated, may hold values from -6 to 6
- w_first: bfloat16 [6, 512, 256], replicated, may hold values from -0.25 to 0.25
- b_first: bfloat16 [6, 256], replicated, may hold values from -4 to 4
- w_second: bfloat16 [6, 256, 256], replicated, may hold values from -0.375 to 0.375
- b_second: bfloat16 [6, 256], replicated, may hold values from -4 to 4
- ln_gain: bfloat16 [6, 256], replicated, may hold values from 0.5 to 1.5
- ln_bias: bfloat16 [6, 256], replicated, may hold values from -4 to 4
- gate_task: bfloat16 [2, 512, 4], replicated, may hold values from -0.5 to 0.5
- gate_task_bias: bfloat16 [2, 4], replicated, may hold values from -1 to 1
- gate_shared: bfloat16 [512, 6], replicated, may hold values from -0.5 to 0.5
- gate_shared_bias: bfloat16 [6], replicated, may hold values from -1 to 1
- cotangent: bfloat16 [3, 32768, 256], P(None, ('wide', 'narrow')), may hold values from -6 to 6
Outputs:
- mixed: bfloat16 [3, 32768, 256], P(None, ('wide', 'narrow'))
- dense_grad: float32 [32768, 384], P(('wide', 'narrow'))
- table_grad: float32 [1024, 16], replicated
- w_first_grad: float32 [6, 512, 256], replicated
- b_first_grad: float32 [6, 256], replicated
- w_second_grad: float32 [6, 256, 256], replicated
- b_second_grad: float32 [6, 256], replicated
- ln_gain_grad: float32 [6, 256], replicated
- ln_bias_grad: float32 [6, 256], replicated
- gate_task_grad: float32 [2, 512, 4], replicated
- gate_task_bias_grad: float32 [2, 4], replicated
- gate_shared_grad: float32 [512, 6], replicated
- gate_shared_bias_grad: float32 [6], replicated
The draws below stay inside these ranges and needn't reach their ends.
All inputs are finite; a program needn't handle non-finite values. No bound on the sum of `presence` on one device may be relied on, other than what follows from the above.
Results may differ from the reference program's by a relative error of at most 0.013.
Values sent between devices are 32-bit elements; how exact they have to be, the bound alone decides.
No kernel may reach another device: no remote copies, remote signals or barrier semaphores. Data moves between devices by JAX's collectives and lax.ppermute only.
A program may use at most 128 MiB of HBM per device.

```python
import math
import jax
import jax.numpy as jnp
import numpy as np
from jax import lax

DENSE = 384
FIELDS = 8
EMB = 16
VOCAB = 1024
HIDDEN_SIZE = 256
OUT = 256
TASKS = 2
SPEC = 2
D_IN = 512
EXPERTS = 6
GATE = 4
EVENTS = 32768


def plant(result, own_key, least, largest):
    longest = result.shape.index(max(result.shape))
    spots = []
    for shift in (0, 1):
        where = [jax.random.randint(jax.random.fold_in(own_key, axis), (), 0, length) for axis, length in enumerate(result.shape)]
        where[longest] = (where[longest] + shift) % result.shape[longest]
        spots.append(tuple(where))
    return result.at[spots[0]].set(least).at[spots[1]].set(largest)


def level_of(rng, extent, cuts, low, high):
    factor_of = 1.0
    for position, blocks in cuts:
        heights = jax.random.uniform(jax.random.fold_in(jax.random.fold_in(rng, 6), position), (blocks,), jnp.float32, low / len(cuts), high / len(cuts))
        factor_of = factor_of * jnp.repeat(jnp.exp(heights), extent[position] // blocks).reshape((-1,) + (1,) * (len(extent) - 1 - position))
    return factor_of


def rank_table(count, lean):
    loads = [(1 << 20) // math.isqrt(rank ** lean) + 1 for rank in range(1, count + 1)]
    width = 1 + sum(loads) // (1 << 30)
    return np.cumsum(np.array([max(1, weight // width) for weight in loads]))


def ranked_ids(key, extent, count, skew):
    grid = rank_table(count, skew)
    pick = jax.random.randint(jax.random.fold_in(key, 1), extent, 0, int(grid[count - 1]))
    rank = jnp.searchsorted(jnp.asarray(grid, jnp.int32), pick, side="right")
    return jax.random.permutation(jax.random.fold_in(key, 2), count)[rank].astype(jnp.int32)


def normal_values(rng, dims, spread, reach, cuts=(), dtype=jnp.bfloat16):
    drawn = jax.random.normal(rng, dims, jnp.float32) * spread
    if len(cuts) > 0:
        drawn = level_of(rng, dims, cuts, -0.22, 0.18) * drawn
    return jnp.clip(drawn, min=-reach, max=reach).astype(dtype)


def setup_inputs(seed: int = 0) -> dict:
    keys = jax.random.split(jax.random.key(seed), 16)
    return {
        "dense_feats": normal_values(keys[0], (EVENTS, DENSE), 1.0, 6.0, ((0, 32),)),
        "sparse_ids": plant(ranked_ids(keys[1], (EVENTS, FIELDS), VOCAB, 2), jax.random.fold_in(keys[1], 3), 0, VOCAB - 1).astype(jnp.int32),
        "presence": plant((jax.random.randint(keys[2], (EVENTS, FIELDS), 0, 4) < 3).astype(jnp.int32), jax.random.fold_in(keys[2], 1), 0, 1),
        "embed_table": normal_values(keys[3], (VOCAB, EMB), 1.0, 6.0),
        "w_first": normal_values(keys[4], (EXPERTS, D_IN, HIDDEN_SIZE), D_IN ** -0.5, 0.25),
        "b_first": normal_values(keys[5], (EXPERTS, HIDDEN_SIZE), 0.3, 4.0),
        "w_second": normal_values(keys[6], (EXPERTS, HIDDEN_SIZE, OUT), HIDDEN_SIZE ** -0.5, 0.375),
        "b_second": normal_values(keys[7], (EXPERTS, OUT), 0.3, 4.0),
        "ln_gain": jnp.clip(1.0 + 0.1 * jax.random.normal(keys[8], (EXPERTS, OUT), jnp.float32), 0.5, 1.5).astype(jnp.bfloat16),
        "ln_bias": normal_values(keys[9], (EXPERTS, OUT), 0.3, 4.0),
        "gate_task": normal_values(keys[10], (TASKS, D_IN, GATE), 0.035, 0.5),
        "gate_task_bias": normal_values(keys[11], (TASKS, GATE), 0.075, 1.0),
        "gate_shared": normal_values(keys[12], (D_IN, EXPERTS), 0.035, 0.5),
        "gate_shared_bias": normal_values(keys[13], (EXPERTS,), 0.075, 1.0),
        "cotangent": normal_values(keys[14], (TASKS + 1, EVENTS, OUT), 1.0, 6.0, ((1, 32),)),
    }


@jax.custom_vjp
def low(v):
    return lax.optimization_barrier(v.astype(jnp.bfloat16)).astype(jnp.float32)

@jax.custom_vjp
def low_back(v):
    return v

def low_keep(v):
    return (low(v), None)

def low_pass(kept, grad):
    return (grad,)

def back_keep(v):
    return (v, None)

def back_low(kept, grad):
    return (low(grad),)
low.defvjp(low_keep, low_pass)
low_back.defvjp(back_keep, back_low)
epsilon = 1e-05

def normalize(values):
    center = values - lax.optimization_barrier(jnp.mean(values, axis=-1, keepdims=True))
    variance = lax.optimization_barrier(jnp.mean(center * center, axis=-1, keepdims=True))
    return center * lax.rsqrt(variance + epsilon)

def layer(dense_part, ids_blk, mask_blk, param_set):
    embed_table, w_first, b_first, w_second, b_second, ln_gain, ln_bias, gate_task, gate_task_bias, gate_shared, gate_shared_bias = param_set
    row_count = dense_part.shape[0]
    looked = jnp.take(embed_table, ids_blk, axis=0) * mask_blk.astype(jnp.float32)[:, :, None]
    features = low(jnp.concatenate([dense_part, looked.reshape(row_count, FIELDS * EMB)], axis=1))
    highest = lax.Precision.HIGHEST
    first_pre = low_back(jnp.einsum('nd,edh->enh', features, w_first, precision=highest) + b_first[:, None, :])
    hidden = low(jax.nn.silu(first_pre))
    second_pre = low_back(jnp.einsum('enh,eho->eno', hidden, w_second, precision=highest) + b_second[:, None, :])
    expert_out = normalize(second_pre) * ln_gain[:, None, :] + ln_bias[:, None, :]
    shared_out = expert_out[TASKS * SPEC:]
    results = []
    for task_index in range(TASKS):
        logits = low_back(jnp.dot(features, gate_task[task_index], precision=highest) + gate_task_bias[task_index])
        weights = jax.nn.softmax(logits, axis=-1)
        chosen = jnp.concatenate([expert_out[task_index * SPEC:(task_index + 1) * SPEC], shared_out], axis=0)
        results.append(jnp.einsum('ne,eno->no', weights, chosen, precision=highest))
    logits = low_back(jnp.dot(features, gate_shared, precision=highest) + gate_shared_bias)
    weights = jax.nn.softmax(logits, axis=-1)
    results.append(jnp.einsum('ne,eno->no', weights, expert_out, precision=highest))
    return jnp.stack(results)

def reference(dense_feats, sparse_ids, presence, embed_table, w_first, b_first, w_second, b_second, ln_gain, ln_bias, gate_task, gate_task_bias, gate_shared, gate_shared_bias, cotangent):
    param_set = tuple((entry.astype(jnp.float32) for entry in (embed_table, w_first, b_first, w_second, b_second, ln_gain, ln_bias, gate_task, gate_task_bias, gate_shared, gate_shared_bias)))
    block_rows = math.gcd(EVENTS, 4096)
    pieces = (dense_feats.reshape(-1, block_rows, DENSE), sparse_ids.reshape(-1, block_rows, FIELDS), presence.reshape(-1, block_rows, FIELDS), cotangent.reshape(TASKS + 1, -1, block_rows, OUT).transpose(1, 0, 2, 3))

    def one_block(totals, block_piece):
        dense_blk, ids_blk, mask_blk, cot_blk = block_piece

        def local_layer(dense_part, params_now):
            return layer(dense_part, ids_blk, mask_blk, params_now)
        mixed_blk, pullback = jax.vjp(local_layer, dense_blk.astype(jnp.float32), param_set)
        grad_dense, grad_params = pullback(cot_blk.astype(jnp.float32))
        return (jax.tree.map(jnp.add, totals, grad_params), (mixed_blk.astype(jnp.bfloat16), grad_dense))
    zero_grads = jax.tree.map(jnp.zeros_like, param_set)
    totals, (mixed, dense_grad) = lax.scan(one_block, zero_grads, pieces)
    mixed = mixed.transpose(1, 0, 2, 3).reshape(TASKS + 1, EVENTS, OUT)
    dense_grad = dense_grad.reshape(EVENTS, DENSE)
    grad_scale = 1.0 / math.sqrt(EVENTS)
    grads = tuple((entry * grad_scale for entry in totals))
    return (mixed, dense_grad, grads[0], grads[1], grads[2], grads[3], grads[4], grads[5], grads[6], grads[7], grads[8], grads[9], grads[10])
```

```python
import functools
import math

import jax
import jax.numpy as jnp
from jax import lax
from jax.experimental import pallas as pl
from jax.experimental.pallas import tpu as pltpu
from jax.sharding import PartitionSpec as P

f32 = jnp.float32
bf16 = jnp.bfloat16
epsilon = 1e-05
LANES = 128
SHARDS = 32
MIB = 1 << 20
BOTH = ("wide", "narrow")
SPANS = ((0, 2), (2, 4), (4, 6))
ORDERS = ("cxy12", "cy12x", "c12xy")


def dot(a, b):
    return lax.dot_general(a, b, (((1,), (0,)), ((), ())), preferred_element_type=f32)


def dot_nt(a, b):
    return lax.dot_general(a, b, (((1,), (1,)), ((), ())), preferred_element_type=f32)


def dot_tn(a, b):
    return lax.dot_general(a, b, (((0,), (0,)), ((), ())), preferred_element_type=f32)


def iota(shape, axis):
    return lax.broadcasted_iota(jnp.int32, shape, axis)


def ones_where(condition):
    return jnp.where(condition, 1.0, 0.0).astype(bf16)


class Sizes:
    def __init__(self, dense, ids, table, w_first, w_second, gate_task):
        self.rows, self.dense = dense.shape
        self.fields = ids.shape[1]
        self.vocab, self.emb = table.shape
        self.experts, self.d_in, self.hidden = w_first.shape
        self.out = w_second.shape[2]
        self.tasks, _, self.gate = gate_task.shape
        self.spec = (self.experts - self.gate) // (self.tasks - 1)
        self.chunk = min(256, self.rows)
        self.chunks = self.rows // self.chunk
        self.low = LANES // self.emb
        self.high = self.vocab // self.low
        self.columns = gate_columns(self.experts, self.tasks, self.spec)
        self.width = self.tasks * self.gate + self.experts
        self.first_rows = self.d_in // SHARDS
        self.second_rows = self.hidden // SHARDS
        self.halves = self.out // LANES
        self.expert_rows = (self.first_rows + self.second_rows) * self.halves
        self.sum_rows = 4 * self.halves
        self.gate_rows = 16 * (self.d_in // LANES)
        self.gate_at = self.high
        self.sums_at = self.gate_at + self.gate_rows
        self.bias_at = self.sums_at + self.experts * self.sum_rows
        self.small_rows = -(-(self.bias_at + 1) // (8 * SHARDS)) * 8

    def piece_rows(self, index):
        last = index == len(SPANS) - 1
        lo, hi = SPANS[index]
        return (hi - lo) * self.expert_rows + (self.small_rows if last else 0)


def gate_columns(experts, tasks, spec):
    shared = tasks * spec
    gate = spec + experts - shared
    columns = []
    for e in range(experts):
        found = []
        for k in range(tasks):
            if e >= shared:
                found.append((k, k * gate + spec + e - shared))
            elif e // spec == k:
                found.append((k, k * gate + e - k * spec))
        found.append((tasks, tasks * gate + e))
        columns.append(found)
    return columns


def gate_matrix(z, gate_task_ref, gate_shared_ref):
    total = None
    for k in range(z.tasks + 1):
        mat = gate_task_ref[k] if k < z.tasks else gate_shared_ref[...]
        n = mat.shape[1]
        place = ones_where(iota((n, LANES), 1) == iota((n, LANES), 0) + k * z.gate)
        part = dot(mat, place)
        total = part if total is None else total + part
    return total.astype(bf16)


def gate_bias(z, task_ref, shared_ref):
    total = None
    for k in range(z.tasks + 1):
        row = task_ref[k : k + 1, :] if k < z.tasks else shared_ref[...]
        n = row.shape[1]
        place = ones_where(iota((n, LANES), 1) == iota((n, LANES), 0) + k * z.gate)
        part = dot(row, place)
        total = part if total is None else total + part
    return total


def gate_lanes(z, k, shape):
    lane = iota(shape, 1)
    first = k * z.gate
    last = first + (z.gate if k < z.tasks else z.experts)
    return (lane >= first) & (lane < last)


def spread_matrix(z, f):
    a = iota((LANES, LANES), 0)
    b = iota((LANES, LANES), 1)
    return ones_where(b == f * z.emb + lax.rem(a, z.emb))


def table_block(z, table_ref):
    total = None
    for low in range(z.low):
        place = ones_where(iota((z.emb, LANES), 1) == iota((z.emb, LANES), 0) + low * z.emb)
        part = dot(table_ref[low * z.high : (low + 1) * z.high, :], place)
        total = part if total is None else total + part
    return total.astype(bf16)


def features_part(z, rows, block, spreads, ids_ref, presence_ref, dense_ref, features_ref):
    ids = ids_ref[rows, :]
    row = jnp.where(presence_ref[rows, :] > 0, lax.rem(ids, z.high), -1)
    low = lax.div(ids, z.high)
    lane_high = iota((z.chunk, z.high), 1)
    lane_low = lax.div(iota((z.chunk, LANES), 1), z.emb)
    total = None
    for f in range(z.fields):
        found = dot(ones_where(row[:, f : f + 1] == lane_high), block)
        kept = jnp.where(low[:, f : f + 1] == lane_low, found, 0.0).astype(bf16)
        part = dot(kept, spreads[f])
        total = part if total is None else total + part
    features_ref[rows, : z.dense] = dense_ref[rows, :]
    features_ref[rows, z.dense :] = total.astype(bf16)


def softmax_part(z, logits):
    result = None
    for k in range(z.tasks + 1):
        lanes = gate_lanes(z, k, logits.shape)
        top = jnp.max(jnp.where(lanes, logits, -jnp.inf), axis=1, keepdims=True)
        value = jnp.exp(jnp.where(lanes, logits - top, -jnp.inf))
        value = value / jnp.sum(value, axis=1, keepdims=True)
        result = value if result is None else result + value
    return result


def logit_part(z, weights, along):
    product = weights * along
    total = jnp.zeros_like(product)
    for k in range(z.tasks + 1):
        lanes = gate_lanes(z, k, product.shape)
        found = jnp.sum(jnp.where(lanes, product, 0.0), axis=1, keepdims=True)
        total = jnp.where(lanes, found, total)
    return (weights * (along - total)).astype(bf16)


def table_part(z, rows, embed, spreads, ids_ref, presence_ref):
    ids = ids_ref[rows, :]
    row = jnp.where(presence_ref[rows, :] > 0, lax.rem(ids, z.high), -1)
    low = lax.div(ids, z.high)
    lane_high = iota((z.chunk, z.high), 1)
    lane_low = lax.div(iota((z.chunk, LANES), 1), z.emb)
    hots = []
    kept = []
    for f in range(z.fields):
        hots.append(ones_where(row[:, f : f + 1] == lane_high))
        wide = dot_nt(embed, spreads[f])
        kept.append(jnp.where(low[:, f : f + 1] == lane_low, wide, 0.0).astype(bf16))
    return dot_tn(jnp.concatenate(hots, axis=0), jnp.concatenate(kept, axis=0))


def experts_kernel(z, index, *refs):
    first = index == 0
    last = index == len(SPANS) - 1
    span = SPANS[index]
    n = span[1] - span[0]
    refs = list(refs)

    def take(count):
        return [refs.pop(0) for _ in range(count)]

    (place_ref,) = take(1)
    w_first_ref, b_first_ref, w_second_ref, b_second_ref, gain_ref, bias_ref, cot_ref = take(7)
    if first:
        dense_ref, ids_ref, presence_ref, table_ref = take(4)
        gate_task_ref, gate_task_bias_ref, gate_shared_ref, gate_shared_bias_ref = take(4)
    else:
        features_ref, weights_ref, part_ref = take(3)
    if last:
        ids_ref, presence_ref, gate_task_ref, gate_shared_ref = take(4)
        earlier_refs = take(index)
    packed_ref, normed_ref, first_ref = take(3)
    if first:
        features_ref, weights_ref = take(2)
    if last:
        (logit_ref,) = take(1)
    else:
        out_ref, sums_ref = take(2)
    hidden_s, second_s, total_s, sums_s = take(4)
    if last:
        gate_s, small_s = take(2)
    if first:
        block = table_block(z, table_ref)
        gates_bias = gate_bias(z, gate_task_bias_ref, gate_shared_bias_ref)
    if first or last:
        spreads = [spread_matrix(z, f) for f in range(z.fields)]
        gates = gate_matrix(z, gate_task_ref, gate_shared_ref)
    sums_s[...] = jnp.zeros_like(sums_s)
    if last:
        gate_s[...] = jnp.zeros_like(gate_s)
        small_s[...] = jnp.zeros_like(small_s)
    scale = 1.0 / z.out

    def step(at, carry):
        rows = pl.ds(pl.multiple_of(at * z.chunk, z.chunk), z.chunk)
        if first:
            features_part(
                z, rows, block, spreads, ids_ref, presence_ref, dense_ref, features_ref
            )
            weights_ref[rows, :] = softmax_part(z, dot(features_ref[rows, :], gates) + gates_bias)
        features = features_ref[rows, :]
        weights = weights_ref[rows, :]
        along = jnp.zeros((z.chunk, LANES), f32) if first else part_ref[0, rows, :]
        embed = jnp.zeros((z.chunk, LANES), f32) if first else part_ref[1, rows, :]
        lane = iota((z.chunk, LANES), 1)
        cots = [cot_ref[k, rows, :].astype(f32) for k in range(z.tasks + 1)]
        for i in range(n):
            e = span[0] + i

            def row(ref):
                return ref[e : e + 1, :].astype(f32)

            gain = row(gain_ref)
            pre = dot(features, w_first_ref[i]) + row(b_first_ref)
            sig = 0.5 * jnp.tanh(0.5 * pre) + 0.5
            hidden = (pre * sig).astype(bf16)
            hidden_s[i, rows, :] = hidden
            second = dot(hidden, w_second_ref[i]) + row(b_second_ref)
            center = second - jnp.sum(second, axis=1, keepdims=True) * scale
            inverse = lax.rsqrt(jnp.sum(center * center, axis=1, keepdims=True) * scale + epsilon)
            normed = center * inverse
            normed_ref[i, rows, :] = normed.astype(bf16)
            expert_out = normed * gain + row(bias_ref)
            upstream = None
            for k, column in z.columns[e]:
                part = weights[:, column : column + 1] * cots[k]
                upstream = part if upstream is None else upstream + part
                found = jnp.sum(cots[k] * expert_out, axis=1, keepdims=True)
                along = jnp.where(lane == column, found, along)
            scaled = upstream * gain
            mean = jnp.sum(scaled, axis=1, keepdims=True) * scale
            mean_normed = jnp.sum(scaled * normed, axis=1, keepdims=True) * scale
            second_grad = (inverse * (scaled - mean - normed * mean_normed)).astype(bf16)
            second_s[i, rows, :] = second_grad
            hidden_grad = dot_nt(second_grad, w_second_ref[i])
            first_grad = (hidden_grad * (sig * (1.0 + pre * (1.0 - sig)))).astype(bf16)
            first_ref[i, rows, :] = first_grad
            embed = embed + dot_nt(first_grad, w_first_ref[i, z.dense :, :])

            def eights(v):
                return jnp.sum(v.reshape(z.chunk // 8, 8, z.out), axis=0)

            sums_s[i, 0] += eights(first_grad.astype(f32))
            sums_s[i, 1] += eights(second_grad.astype(f32))
            sums_s[i, 2] += eights(upstream * normed)
            sums_s[i, 3] += eights(upstream)
        if not last:
            out_ref[0, rows, :] = along
            out_ref[1, rows, :] = embed
            return carry
        logit_grad = logit_part(z, weights, along)
        logit_ref[rows, :] = logit_grad
        gate_s[...] += dot_tn(logit_grad, features)
        embed = embed + dot_nt(logit_grad, gates[z.dense :, :])
        small_s[: z.high, :] += table_part(
            z, rows, embed.astype(bf16), spreads, ids_ref, presence_ref
        )
        small_s[z.bias_at : z.bias_at + 1, :] += jnp.sum(
            logit_grad.astype(f32), axis=0, keepdims=True
        )
        return carry

    lax.fori_loop(0, z.chunks, step, 0)

    for i in range(n):
        for q in range(4):
            found = jnp.sum(sums_s[i, q], axis=0, keepdims=True)
            for h in range(z.halves):
                line = i * z.sum_rows + q * z.halves + h
                part = found[:, h * LANES : (h + 1) * LANES]
                if last:
                    line = z.sums_at + span[0] * z.sum_rows + line
                    small_s[line : line + 1, :] = part
                else:
                    sums_ref[line : line + 1, :] = part
    if last:
        line = z.sums_at
        for ref in earlier_refs:
            small_s[line : line + ref.shape[0], :] = ref[...]
            line += ref.shape[0]
        for q in range(z.d_in // LANES):
            line = z.gate_at + q * 16
            small_s[line : line + 16, :] = gate_s[:16, q * LANES : (q + 1) * LANES]

    place = place_ref[index]
    for i in range(n):
        total_s[i, : z.d_in, :] = dot_tn(features_ref[...], first_ref[i])
        total_s[i, z.d_in :, :] = dot_tn(hidden_s[i], second_s[i])

    def pack(r, carry):
        block = lax.bitwise_xor(r, place)
        for i in range(n):
            line = i * z.expert_rows
            for start, count in ((0, z.first_rows), (z.d_in, z.second_rows)):
                lines = pl.ds(pl.multiple_of(start + block * count, 8), count)
                for h in range(z.halves):
                    packed_ref[r, line : line + count, :] = total_s[
                        i, lines, h * LANES : (h + 1) * LANES
                    ]
                    line += count
        if last:
            lines = pl.ds(pl.multiple_of(block * z.small_rows, 8), z.small_rows)
            packed_ref[r, n * z.expert_rows :, :] = small_s[lines, :]
        return carry

    lax.fori_loop(0, SHARDS, pack, 0)


def outputs_kernel(z, *refs):
    refs = list(refs)
    weights_ref, logit_ref, w_first_ref, gain_ref, bias_ref, gate_task_ref, gate_shared_ref = refs[
        :7
    ]
    normed_refs = refs[7 : 7 + len(SPANS)]
    first_refs = refs[7 + len(SPANS) : 7 + 2 * len(SPANS)]
    mixed_ref, dense_ref = refs[7 + 2 * len(SPANS) :]
    weights = weights_ref[...]
    mixed = [None] * (z.tasks + 1)
    gates = gate_matrix(z, gate_task_ref, gate_shared_ref)
    dense = dot_nt(logit_ref[...], gates[: z.dense, :])
    for index, span in enumerate(SPANS):
        for i in range(span[1] - span[0]):
            e = span[0] + i
            expert_out = normed_refs[index][i].astype(f32) * gain_ref[e : e + 1, :].astype(
                f32
            ) + bias_ref[e : e + 1, :].astype(f32)
            for k, column in z.columns[e]:
                part = weights[:, column : column + 1] * expert_out
                mixed[k] = part if mixed[k] is None else mixed[k] + part
            dense = dense + dot_nt(first_refs[index][i], w_first_ref[e, : z.dense, :])
    for k in range(z.tasks + 1):
        mixed_ref[k] = mixed[k].astype(bf16)
    dense_ref[...] = dense


def unpack_kernel(z, group, grad_scale, place_ref, *refs):
    pieces = refs[: len(SPANS)]
    small_ref = refs[len(SPANS)]
    w_first_ref, w_second_ref = refs[len(SPANS) + 1 : len(SPANS) + 3]
    table_ref, gate_task_ref, gate_shared_ref, gate_bias_ref = refs[len(SPANS) + 3 :][:4]
    sum_refs = refs[len(SPANS) + 7 :][:4]
    small_s = refs[-1]
    for index, span in enumerate(SPANS):
        low_bits = lax.bitwise_and(place_ref[index], group - 1)
        for j in range(group):
            block = lax.bitwise_xor(low_bits, j)
            line = 0
            for e in range(*span):
                for ref, count in ((w_first_ref, z.first_rows), (w_second_ref, z.second_rows)):
                    for h in range(z.halves):
                        ref[e, j * count : (j + 1) * count, h * LANES : (h + 1) * LANES] = (
                            pieces[index][block, line : line + count, :] * grad_scale
                        )
                        line += count

    @pl.when(pl.program_id(0) == 0)
    def _():
        place = place_ref[len(SPANS) - 1]
        for a in range(SHARDS):
            small_s[a * z.small_rows : (a + 1) * z.small_rows, :] = (
                small_ref[lax.bitwise_xor(place, a)] * grad_scale
            )
        for low in range(z.low):
            table_ref[low * z.high : (low + 1) * z.high, :] = small_s[
                : z.high, low * z.emb : (low + 1) * z.emb
            ]
        for q in range(z.d_in // LANES):
            line = z.gate_at + q * 16
            found = small_s[line : line + 16, :].T
            lines = slice(q * LANES, (q + 1) * LANES)
            for k in range(z.tasks):
                gate_task_ref[k, lines, :] = found[:, k * z.gate : (k + 1) * z.gate]
            gate_shared_ref[lines, :] = found[:, z.tasks * z.gate : z.width]
        gate_bias_ref[...] = small_s[z.bias_at : z.bias_at + 1, :]
        for e in range(z.experts):
            for q in range(4):
                for h in range(z.halves):
                    line = z.sums_at + e * z.sum_rows + q * z.halves + h
                    sum_refs[q][e : e + 1, h * LANES : (h + 1) * LANES] = small_s[
                        line : line + 1, :
                    ]


VMEM = pl.BlockSpec(memory_space=pltpu.VMEM)
SMEM = pl.BlockSpec(memory_space=pltpu.SMEM)


def shape_of(shape, dtype=f32):
    return jax.ShapeDtypeStruct(shape, dtype)


def run_experts(z, index, places, params, cotangent, extra, earlier):
    first = index == 0
    last = index == len(SPANS) - 1
    span = SPANS[index]
    n = span[1] - span[0]
    w_first, b_first, w_second, b_second, gain, bias = params

    def experts_block(array):
        return pl.BlockSpec(
            (n,) + array.shape[1:], lambda at: (span[0] // n, 0, 0), memory_space=pltpu.VMEM
        )

    def whole(array):
        return pl.BlockSpec(array.shape, lambda at: (0,) * array.ndim, memory_space=pltpu.VMEM)

    operands = [places, w_first, b_first, w_second, b_second, gain, bias, cotangent]
    operands += list(extra) + list(earlier)
    in_specs = [SMEM] + [
        experts_block(v) if v is w_first or v is w_second else whole(v) for v in operands[1:]
    ]
    rows = z.rows
    out_shape = [
        shape_of((SHARDS, z.piece_rows(index), LANES)),
        shape_of((n, rows, z.out), bf16),
        shape_of((n, rows, z.hidden), bf16),
    ]
    if first:
        out_shape += [shape_of((rows, z.d_in), bf16), shape_of((rows, LANES))]
    if last:
        out_shape += [shape_of((rows, LANES), bf16)]
    else:
        out_shape += [shape_of((2, rows, LANES)), shape_of((n * z.sum_rows, LANES))]
    scratch = [
        pltpu.VMEM((n, rows, z.hidden), bf16),
        pltpu.VMEM((n, rows, z.out), bf16),
        pltpu.VMEM((n, z.d_in + z.hidden, z.out), f32),
        pltpu.VMEM((n, 4, 8, z.out), f32),
    ]
    if last:
        scratch += [
            pltpu.VMEM((LANES, z.d_in), f32),
            pltpu.VMEM((z.small_rows * SHARDS, LANES), f32),
        ]
    macs = rows * n * 3 * (z.d_in * z.hidden + z.hidden * z.out)
    return pl.pallas_call(
        functools.partial(experts_kernel, z, index),
        grid=(1,),
        in_specs=in_specs,
        out_specs=[whole(v) for v in out_shape],
        out_shape=out_shape,
        scratch_shapes=scratch,
        compiler_params=pltpu.CompilerParams(vmem_limit_bytes=48 * MIB),
        cost_estimate=pl.CostEstimate(
            flops=2 * macs, bytes_accessed=6 * MIB, transcendentals=rows * n * z.hidden
        ),
        name="experts_%d" % index,
    )(*operands)


def run_outputs(z, weights, logit_grad, w_first, gain, bias, gates, normed, firsts):
    block = z.chunk

    def whole(array):
        return pl.BlockSpec(array.shape, lambda at: (0,) * array.ndim)

    def rows_of(array):
        if array.ndim == 2:
            return pl.BlockSpec((block, array.shape[1]), lambda at: (at, 0))
        return pl.BlockSpec((array.shape[0], block, array.shape[2]), lambda at: (0, at, 0))

    out_shape = [shape_of((z.tasks + 1, z.rows, z.out), bf16), shape_of((z.rows, z.dense))]
    return pl.pallas_call(
        functools.partial(outputs_kernel, z),
        grid=(z.rows // block,),
        in_specs=[rows_of(weights), rows_of(logit_grad)]
        + [whole(v) for v in (w_first, gain, bias) + gates]
        + [rows_of(v) for v in normed + firsts],
        out_specs=[rows_of(v) for v in out_shape],
        out_shape=out_shape,
        compiler_params=pltpu.CompilerParams(vmem_limit_bytes=32 * MIB),
        cost_estimate=pl.CostEstimate(
            flops=2 * z.rows * z.experts * z.hidden * z.dense,
            bytes_accessed=11 * MIB,
            transcendentals=0,
        ),
        name="outputs",
    )(weights, logit_grad, w_first, gain, bias, *gates, *normed, *firsts)


def run_unpack(z, places, pieces, grad_scale):
    group = 4
    steps = SHARDS // group

    def piece_spec(index):
        rows = (SPANS[index][1] - SPANS[index][0]) * z.expert_rows
        return pl.BlockSpec(
            (group, rows, LANES),
            lambda at, place: (lax.bitwise_xor(at, lax.div(place[index], group)), 0, 0),
        )

    small = pieces[-1][:, -z.small_rows :, :]

    def whole(array):
        return pl.BlockSpec(array.shape, lambda at, place: (0,) * array.ndim)

    out_shape = [
        shape_of((z.experts, z.d_in, z.hidden)),
        shape_of((z.experts, z.hidden, z.out)),
        shape_of((z.vocab, z.emb)),
        shape_of((z.tasks, z.d_in, z.gate)),
        shape_of((z.d_in, z.experts)),
        shape_of((1, LANES)),
    ] + [shape_of((z.experts, z.out))] * 4

    def sharded(array):
        return pl.BlockSpec(
            (array.shape[0], array.shape[1] // steps, array.shape[2]), lambda at, place: (0, at, 0)
        )

    pieces = [v if v.shape[1] % z.expert_rows == 0 else v[:, : -z.small_rows] for v in pieces]
    return pl.pallas_call(
        functools.partial(unpack_kernel, z, group, grad_scale),
        grid_spec=pltpu.PrefetchScalarGridSpec(
            num_scalar_prefetch=1,
            grid=(steps,),
            in_specs=[piece_spec(i) for i in range(len(SPANS))] + [whole(small)],
            out_specs=[sharded(out_shape[0]), sharded(out_shape[1])]
            + [whole(v) for v in out_shape[2:]],
            scratch_shapes=[pltpu.VMEM((z.small_rows * SHARDS, LANES), f32)],
        ),
        out_shape=out_shape,
        compiler_params=pltpu.CompilerParams(vmem_limit_bytes=32 * MIB),
        cost_estimate=pl.CostEstimate(flops=0, bytes_accessed=10 * MIB, transcendentals=0),
        name="unpack",
    )(places, *pieces, small)


class Ring:
    FLIPS = {"c": 1, "x": 2, "y": 4, "1": 8, "2": 16}

    def __init__(self, fits):
        self.fits = fits

    def exchange(self, value, axis):
        flip = self.FLIPS[axis]
        return lax.ppermute(value, BOTH, [(i, i ^ flip) for i in range(SHARDS)])

    def place(self, order):
        if not self.fits:
            return jnp.int32(0)
        device = lax.axis_index("wide") * 4 + lax.axis_index("narrow")
        result = jnp.int32(0)
        for axis in order:
            bit = lax.rem(lax.div(device, self.FLIPS[axis]), 2)
            result = result * 2 + bit
        return result

    def reduce(self, pieces):
        if not self.fits:
            return lax.psum(pieces, BOTH)
        pieces = list(pieces)
        for stage in range(5):
            halves = [v.shape[0] // 2 for v in pieces]
            got = [
                self.exchange(v[h:], order[stage])
                for v, h, order in zip(pieces, halves, ORDERS)
            ]
            pieces = [v[:h] + g for v, h, g in zip(pieces, halves, got)]
        for stage in reversed(range(5)):
            got = [self.exchange(v, order[stage]) for v, order in zip(pieces, ORDERS)]
            pieces = [jnp.concatenate([v, g], axis=0) for v, g in zip(pieces, got)]
        return pieces


def local(
    fits,
    dense_feats,
    sparse_ids,
    presence,
    embed_table,
    w_first,
    b_first,
    w_second,
    b_second,
    ln_gain,
    ln_bias,
    gate_task,
    gate_task_bias,
    gate_shared,
    gate_shared_bias,
    cotangent,
):
    z = Sizes(dense_feats, sparse_ids, embed_table, w_first, w_second, gate_task)
    ring = Ring(fits)
    places = jnp.stack([ring.place(order) for order in ORDERS])
    params = (w_first, b_first, w_second, b_second, ln_gain, ln_bias)
    pieces, normed, firsts, sums = [], [], [], []
    extra = (
        dense_feats,
        sparse_ids,
        presence,
        embed_table,
        gate_task,
        gate_task_bias,
        gate_shared,
        gate_shared_bias.reshape(1, -1),
    )
    for index in range(len(SPANS)):
        last = index == len(SPANS) - 1
        found = run_experts(
            z, index, places, params, cotangent, extra, sums if last else []
        )
        pieces.append(found[0])
        normed.append(found[1])
        firsts.append(found[2])
        rest = found[3:]
        if index == 0:
            features, weights = rest[:2]
            rest = rest[2:]
        if last:
            logit_grad = rest[0]
        else:
            part, sum_rows = rest
            sums.append(sum_rows)
            extra = (features, weights, part)
            if index == len(SPANS) - 2:
                extra += (sparse_ids, presence, gate_task, gate_shared)
    pieces = ring.reduce(pieces)
    mixed, dense_grad = run_outputs(
        z, weights, logit_grad, w_first, ln_gain, ln_bias, (gate_task, gate_shared), normed, firsts
    )
    total_rows = z.rows * lax.axis_size("wide") * lax.axis_size("narrow")
    grads = run_unpack(z, places, pieces, 1.0 / math.sqrt(total_rows))
    w_first_grad, w_second_grad, table_grad, gate_task_grad, gate_shared_grad, bias_row = grads[:6]
    b_first_grad, b_second_grad, gain_grad, bias_grad = grads[6:]
    task_width = z.tasks * z.gate
    return (
        mixed,
        dense_grad,
        table_grad,
        w_first_grad,
        b_first_grad,
        w_second_grad,
        b_second_grad,
        gain_grad,
        bias_grad,
        gate_task_grad,
        bias_row[0, :task_width].reshape(z.tasks, z.gate),
        gate_shared_grad,
        bias_row[0, task_width : z.width],
    )


def solution(mesh):
    fits = (mesh.shape["wide"], mesh.shape["narrow"]) == (8, 4)
    rows = P(BOTH, None)
    middle = P(None, BOTH, None)
    return jax.shard_map(
        functools.partial(local, fits),
        mesh=mesh,
        in_specs=(rows, rows, rows) + (P(),) * 11 + (middle,),
        out_specs=(middle, rows) + (P(),) * 11,
        check_vma=False,
    )
```

```python
import functools
import math

import jax
import jax.numpy as jnp
from jax import lax
from jax.experimental import pallas as pl
from jax.experimental.pallas import tpu as pltpu
from jax.sharding import PartitionSpec as P

f32 = jnp.float32
bf16 = jnp.bfloat16
epsilon = 1e-05
LANES = 128
DEVICES = 32
MIB = 1 << 20
LAG = 2
BOTH = ("wide", "narrow")
SPANS = ((0, 2), (2, 4), (4, 6))
FLIPS = {"c": 1, "x": 2, "y": 4, "1": 8, "2": 16}
AXES = "xy1"
ORDERS = ("xy1", "y1x", "1xy")
HALVED = len(AXES)
BLOCKS = 2 << HALVED


def dot(a, b):
    return lax.dot_general(a, b, (((1,), (0,)), ((), ())), preferred_element_type=f32)


def dot_nt(a, b):
    return lax.dot_general(a, b, (((1,), (1,)), ((), ())), preferred_element_type=f32)


def dot_tn(a, b):
    return lax.dot_general(a, b, (((0,), (0,)), ((), ())), preferred_element_type=f32)


def iota(shape, axis):
    return lax.broadcasted_iota(jnp.int32, shape, axis)


def ones_where(condition):
    return jnp.where(condition, 1.0, 0.0).astype(bf16)


class Sizes:
    def __init__(self, dense, ids, table, w_first, w_second, gate_task):
        self.rows, self.dense = dense.shape
        self.fields = ids.shape[1]
        self.vocab, self.emb = table.shape
        self.experts, self.d_in, self.hidden = w_first.shape
        self.out = w_second.shape[2]
        self.tasks, _, self.gate = gate_task.shape
        self.spec = (self.experts - self.gate) // (self.tasks - 1)
        self.low = LANES // self.emb
        self.high = self.vocab // self.low
        self.columns = gate_columns(self.experts, self.tasks, self.spec)
        self.width = self.tasks * self.gate + self.experts
        self.first_rows = self.d_in // BLOCKS
        self.second_rows = self.hidden // BLOCKS
        self.halves = self.out // LANES
        self.expert_rows = (self.first_rows + self.second_rows) * self.halves
        self.sum_rows = 4 * self.halves
        self.gate_rows = 16 * (self.d_in // LANES)
        self.gate_at = self.high
        self.sums_at = self.gate_at + self.gate_rows
        self.bias_at = self.sums_at + self.experts * self.sum_rows
        self.small_rows = -(-(self.bias_at + 1) // (8 * BLOCKS)) * 8

    def piece_rows(self, index):
        lo, hi = SPANS[index]
        last = index == len(SPANS) - 1
        return (hi - lo) * self.expert_rows + (self.small_rows if last else 0)


def gate_columns(experts, tasks, spec):
    shared = tasks * spec
    gate = spec + experts - shared
    columns = []
    for e in range(experts):
        found = []
        for k in range(tasks):
            if e >= shared:
                found.append((k, k * gate + spec + e - shared))
            elif e // spec == k:
                found.append((k, k * gate + e - k * spec))
        found.append((tasks, tasks * gate + e))
        columns.append(found)
    return columns


def gate_matrix(z, gate_task_ref, gate_shared_ref):
    total = None
    for k in range(z.tasks + 1):
        mat = gate_task_ref[k] if k < z.tasks else gate_shared_ref[...]
        n = mat.shape[0]
        place = ones_where(iota((LANES, n), 0) == iota((LANES, n), 1) + k * z.gate)
        part = dot(place, mat)
        total = part if total is None else total + part
    return total.astype(bf16)


def gate_bias(z, task_ref, shared_ref):
    total = None
    for k in range(z.tasks + 1):
        row = task_ref[k : k + 1, :] if k < z.tasks else shared_ref[...]
        n = row.shape[1]
        place = ones_where(iota((n, LANES), 1) == iota((n, LANES), 0) + k * z.gate)
        part = dot(row, place)
        total = part if total is None else total + part
    return total


def gate_lanes(z, k, shape):
    lane = iota(shape, 1)
    first = k * z.gate
    last = first + (z.gate if k < z.tasks else z.experts)
    return (lane >= first) & (lane < last)


def spread_matrix(z, f):
    a = iota((LANES, LANES), 0)
    b = iota((LANES, LANES), 1)
    return ones_where(b == f * z.emb + lax.rem(a, z.emb))


def table_block(z, table_ref):
    return jnp.concatenate(
        [table_ref[:, low * z.high : (low + 1) * z.high] for low in range(z.low)], axis=0
    )


def split_ids(z, ids_ref, presence_ref):
    ids = ids_ref[...]
    row = jnp.where(presence_ref[...] > 0, lax.bitwise_and(ids, z.high - 1), -1)
    return row, lax.div(ids, z.high)


def turned(v):
    return v.astype(f32).T.astype(jnp.int32)


def lookup_part(z, block, spreads, ids_ref, presence_ref):
    row, low = split_ids(z, ids_ref, presence_ref)
    row, low = turned(row), turned(low)
    lane_high = iota((z.rows, z.high), 1)
    lane_low = lax.div(iota((z.rows, LANES), 1), z.emb)
    total = None
    for f in range(z.fields):
        found = dot_nt(ones_where(row[:, f : f + 1] == lane_high), block)
        kept = jnp.where(low[:, f : f + 1] == lane_low, found, 0.0).astype(bf16)
        part = dot(kept, spreads[f])
        total = part if total is None else total + part
    return total


def softmax_part(z, logits):
    result = None
    for k in range(z.tasks + 1):
        lanes = gate_lanes(z, k, logits.shape)
        top = jnp.max(jnp.where(lanes, logits, -jnp.inf), axis=1, keepdims=True)
        value = jnp.exp(jnp.where(lanes, logits - top, -jnp.inf))
        value = value / jnp.sum(value, axis=1, keepdims=True)
        result = value if result is None else result + value
    return result


def logit_part(z, weights, along):
    product = weights * along
    total = jnp.zeros_like(product)
    for k in range(z.tasks + 1):
        lanes = gate_lanes(z, k, product.shape)
        found = jnp.sum(jnp.where(lanes, product, 0.0), axis=1, keepdims=True)
        total = jnp.where(lanes, found, total)
    return (weights * (along - total)).astype(bf16)


def table_part(z, embed, spreads, ids_ref, presence_ref):
    row, low = split_ids(z, ids_ref, presence_ref)
    low = turned(low)
    line_high = iota((z.high, z.rows), 0)
    lane_low = lax.div(iota((z.rows, LANES), 1), z.emb)
    hots = []
    kept = []
    for f in range(z.fields):
        hots.append(ones_where(row[f : f + 1, :] == line_high))
        wide = dot_nt(embed, spreads[f])
        kept.append(jnp.where(low[:, f : f + 1] == lane_low, wide, 0.0).astype(bf16))
    return dot(jnp.concatenate(hots, axis=1), jnp.concatenate(kept, axis=0))


def device_bits(device):
    own = jnp.int32(0)
    for axis in AXES:
        own = own * 2 + lax.bitwise_and(lax.div(device, FLIPS[axis]), 1)
    return lax.bitwise_and(device, 1), own


def block_of(shard, order, core, own):
    count = BLOCKS // 2
    flips = lax.bitwise_xor(own, shard % count)
    q = jnp.int32(0)
    for axis in order:
        bit = lax.bitwise_and(lax.shift_right_logical(flips, HALVED - 1 - AXES.index(axis)), 1)
        q = q * 2 + bit
    return lax.bitwise_xor(core, shard // count) * count + q


def column_matrix(z, k, ref):
    total = None
    row = iota((LANES, z.out), 0)
    for e in range(z.experts):
        for gate, column in z.columns[e]:
            if gate == k:
                part = jnp.where(row == column, ref[e : e + 1, :].astype(f32), 0.0)
                total = part if total is None else total + part
    return total.astype(bf16)


def main_kernel(z, grad_scale, *refs):
    refs = list(refs)

    def take(count):
        return [refs.pop(0) for _ in range(count)]

    (device_ref,) = take(1)
    far_refs = take(15)
    piece_refs = [take(2) for _ in SPANS]
    normed_ref, first_ref, weights_ref, logit_ref = take(4)
    here = take(15)
    sems, out_sems, features_s, normed_s, first_s, weights_s, logit_s, small_s = take(8)
    packed_s = take(len(SPANS))
    copies = [
        pltpu.make_async_copy(a, b, sems.at[i]) for i, (a, b) in enumerate(zip(far_refs, here))
    ]
    for copy in copies:
        copy.start()
    sent = []

    def send(source, target):
        copy = pltpu.make_async_copy(source, target, out_sems.at[len(sent)])
        copy.start()
        sent.append(copy)

    core, own = device_bits(device_ref[0])
    ids_ref, presence_ref, table_ref, gate_task_ref, gate_task_bias_ref = here[:5]
    gate_shared_ref, gate_shared_bias_ref, dense_ref, w_first_ref, b_first_ref = here[5:10]
    w_second_ref, b_second_ref, gain_ref, bias_ref, cot_ref = here[10:]
    spreads = [spread_matrix(z, f) for f in range(z.fields)]
    for copy in copies[:3]:
        copy.wait()
    looked = lookup_part(z, table_block(z, table_ref), spreads, ids_ref, presence_ref)
    features_s[:, z.dense :] = (0.5 * looked).astype(bf16)
    for copy in copies[3:8]:
        copy.wait()
    features_s[:, : z.dense] = dense_ref[...] * 0.5
    gates = gate_matrix(z, gate_task_ref, gate_shared_ref)
    features = features_s[...]
    logits = 2.0 * dot_nt(features, gates)
    weights = softmax_part(z, logits + gate_bias(z, gate_task_bias_ref, gate_shared_bias_ref))
    weights_s[...] = weights
    send(weights_s, weights_ref)
    for copy in copies[8:]:
        copy.wait()
    lane = iota((z.rows, LANES), 1)
    along = None
    few = weights.astype(bf16)
    bias_sums = []
    for k in range(z.tasks + 1):
        part = dot_nt(cot_ref[k], column_matrix(z, k, bias_ref))
        along = part if along is None else along + part
        bias_sums.append(dot_tn(few, cot_ref[k]))
    embed = jnp.zeros((z.rows, LANES), f32)
    scale = 1.0 / z.out
    for index, span in enumerate(SPANS):
        for e in range(*span):

            def row(ref):
                return ref[e : e + 1, :].astype(f32)

            def mean(v):
                return jnp.sum(v, axis=1, keepdims=True) * scale

            def keep(q, v):
                for h in range(z.halves):
                    line = z.sums_at + e * z.sum_rows + q * z.halves + h
                    small_s[line : line + 1, :] = v[:, h * LANES : (h + 1) * LANES]

            def total(v):
                return jnp.sum(v, axis=0, keepdims=True)

            gain = row(gain_ref)
            half = dot(features_s[...], w_first_ref[e]) + 0.5 * row(b_first_ref)
            turn = jnp.tanh(half)
            up = 1.0 + turn
            smooth = half * up
            hidden = smooth.astype(bf16)
            second = dot(hidden, w_second_ref[e]) + row(b_second_ref)
            center = second - mean(second)
            inverse = lax.rsqrt(mean(center * center) + epsilon)
            normed = center * inverse
            normed_s[e] = normed.astype(bf16)
            send(normed_s.at[e], normed_ref.at[e])
            gained = normed * gain
            upstream = None
            for k, column in z.columns[e]:
                cot = cot_ref[k].astype(f32)
                part = weights_s[:, column : column + 1] * cot
                upstream = part if upstream is None else upstream + part
                found = jnp.sum(cot * gained, axis=1, keepdims=True)
                along = jnp.where(lane == column, along + found, along)
            product = upstream * normed
            scaled = upstream * gain
            second_grad = inverse * (scaled - mean(scaled) - normed * mean(product * gain))
            keep(1, total(second_grad))
            keep(2, total(product))
            second_grad = second_grad.astype(bf16)
            second_total = dot_tn(hidden, second_grad) * grad_scale
            first_grad = dot_nt(second_grad, w_second_ref[e]) * (up + smooth * (1.0 - turn))
            keep(0, 0.5 * total(first_grad))
            first_s[e] = first_grad.astype(bf16)
            send(first_s.at[e], first_ref.at[e])
            first_total = dot_tn(features_s[...], first_s[e]) * grad_scale
            embed = embed + dot_nt(first_s[e], w_first_ref[e, z.dense :, :])
            found = None
            for k, column in z.columns[e]:
                part = bias_sums[k][column : column + 1, :]
                found = part if found is None else found + part
            keep(3, found)
            line = (e - span[0]) * z.expert_rows
            lines = pl.ds(line, z.expert_rows)
            for shard in range(BLOCKS):
                at = block_of(shard, ORDERS[index], core, own)
                begin = line
                for v, count in ((first_total, z.first_rows), (second_total, z.second_rows)):
                    for h in range(z.halves):
                        packed_s[index][at, begin : begin + count, :] = v[
                            shard * count : (shard + 1) * count, h * LANES : (h + 1) * LANES
                        ]
                        begin += count
            for side in range(2):
                blocks = pl.ds(side * (BLOCKS // 2), BLOCKS // 2)
                send(packed_s[index].at[blocks, lines, :], piece_refs[index][side].at[:, lines, :])
    logit_grad = logit_part(z, weights_s[...], along)
    logit_s[...] = logit_grad
    send(logit_s, logit_ref)
    gate_total = 2.0 * dot_tn(logit_grad, features_s[...])
    embed = 0.5 * embed + dot(logit_grad, gates[:, z.dense :])
    table_total = table_part(z, embed.astype(bf16), spreads, ids_ref, presence_ref)
    small_s[: z.high, :] = table_total.T
    for q in range(z.d_in // LANES):
        line = z.gate_at + q * 16
        small_s[line : line + 16, :] = gate_total[:16, q * LANES : (q + 1) * LANES]
    small_s[z.bias_at :, :] = jnp.zeros_like(small_s[z.bias_at :, :])
    small_s[z.bias_at : z.bias_at + 1, :] = jnp.sum(logit_grad.astype(f32), axis=0, keepdims=True)
    lines = pl.ds((SPANS[-1][1] - SPANS[-1][0]) * z.expert_rows, z.small_rows)
    for shard in range(BLOCKS):
        at = block_of(shard, ORDERS[-1], core, own)
        packed_s[-1][at, lines, :] = (
            small_s[shard * z.small_rows : (shard + 1) * z.small_rows, :] * grad_scale
        )
    for side in range(2):
        blocks = pl.ds(side * (BLOCKS // 2), BLOCKS // 2)
        send(packed_s[-1].at[blocks, lines, :], piece_refs[-1][side].at[:, lines, :])
    for copy in sent:
        copy.wait()


def outputs_kernel(z, *refs):
    weights_ref, logit_ref, w_first_ref, gain_ref, bias_ref, gate_task_ref, gate_shared_ref = refs[
        :7
    ]
    normed_ref, first_ref, mixed_ref, dense_ref = refs[7:]
    weights = weights_ref[...]
    mixed = [None] * (z.tasks + 1)
    gates = gate_matrix(z, gate_task_ref, gate_shared_ref)
    dense = None
    for e in range(z.experts):
        expert_out = normed_ref[e].astype(f32) * gain_ref[e : e + 1, :].astype(f32) + bias_ref[
            e : e + 1, :
        ].astype(f32)
        for k, column in z.columns[e]:
            part = weights[:, column : column + 1] * expert_out
            mixed[k] = part if mixed[k] is None else mixed[k] + part
        part = dot_nt(first_ref[e], w_first_ref[e, : z.dense, :])
        dense = part if dense is None else dense + part
    for k in range(z.tasks + 1):
        mixed_ref[k] = mixed[k].astype(bf16)
    dense_ref[...] = 0.5 * dense + dot(logit_ref[...], gates[:, : z.dense])


def unpack_kernel(z, index, *refs):
    last = index == len(SPANS) - 1
    refs = list(refs)

    def take(count):
        return [refs.pop(0) for _ in range(count)]

    device_ref, near_ref, far_ref = take(3)
    if index:
        take(2)
    w_first_ref, w_second_ref = take(2)
    core, own = device_bits(device_ref[0])
    base = pl.program_id(0) * z.expert_rows
    count = BLOCKS // 2

    def unpack(shard, side, from_ref):
        at = lax.bitwise_and(block_of(shard, ORDERS[index], core, own), count - 1)
        line = 0
        for ref, rows in ((w_first_ref, z.first_rows), (w_second_ref, z.second_rows)):
            for h in range(z.halves):
                lines = pl.ds(pl.multiple_of(base + line, 8), rows)
                ref[0, shard * rows : (shard + 1) * rows, h * LANES : (h + 1) * LANES] = from_ref[
                    at, lines, :
                ]
                line += rows

    for side, from_ref in enumerate((near_ref, far_ref)):
        for owner in range(2):

            @pl.when(lax.bitwise_xor(core, owner) == side)
            def _():
                for shard in range(owner * count, (owner + 1) * count):
                    unpack(shard, side, from_ref)

    if not last:
        return
    table_ref, gate_task_ref, gate_task_bias_ref, gate_shared_ref, gate_shared_bias_ref = take(5)
    sum_refs = take(4)
    (small_s,) = take(1)

    @pl.when(pl.program_id(0) == 0)
    def _():
        start = (SPANS[index][1] - SPANS[index][0]) * z.expert_rows
        for side, from_ref in enumerate((near_ref, far_ref)):
            for owner in range(2):

                @pl.when(lax.bitwise_xor(core, owner) == side)
                def _():
                    for shard in range(owner * count, (owner + 1) * count):
                        at = block_of(shard, ORDERS[index], core, own)
                        small_s[shard * z.small_rows : (shard + 1) * z.small_rows, :] = from_ref[
                            lax.bitwise_and(at, count - 1), start:, :
                        ]

        for low in range(z.low):
            table_ref[:, low * z.high : (low + 1) * z.high] = small_s[
                low * z.emb : (low + 1) * z.emb, :
            ]
        for q in range(z.d_in // LANES):
            line = z.gate_at + q * 16
            lanes = slice(q * LANES, (q + 1) * LANES)
            for k in range(z.tasks):
                gate_task_ref[k, :, lanes] = small_s[
                    line + k * z.gate : line + (k + 1) * z.gate, :
                ]
            gate_shared_ref[:, lanes] = small_s[line + z.tasks * z.gate : line + z.width, :]
        bias_row = small_s[z.bias_at : z.bias_at + 1, :]
        for k in range(z.tasks):
            gate_task_bias_ref[k : k + 1, :] = bias_row[:, k * z.gate : (k + 1) * z.gate]
        gate_shared_bias_ref[...] = bias_row[:, z.tasks * z.gate : z.width]
        for e in range(z.experts):
            for q in range(4):
                for h in range(z.halves):
                    line = z.sums_at + e * z.sum_rows + q * z.halves + h
                    sum_refs[q][e : e + 1, h * LANES : (h + 1) * LANES] = small_s[
                        line : line + 1, :
                    ]


SMEM = pl.BlockSpec(memory_space=pltpu.SMEM)
ANY = pl.BlockSpec(memory_space=pl.ANY)
HBM = pl.BlockSpec(memory_space=pltpu.HBM)


def shape_of(shape, dtype=f32):
    return jax.ShapeDtypeStruct(shape, dtype)


def whole(array):
    return pl.BlockSpec(array.shape, lambda at: (0,) * len(array.shape))


def rows_spec(z, block, shape):
    if shape == (z.fields, z.rows):
        return pl.BlockSpec((z.fields, block), lambda at: (0, at))
    if len(shape) == 2:
        return pl.BlockSpec((block, shape[1]), lambda at: (at, 0))
    return pl.BlockSpec((shape[0], block, shape[2]), lambda at: (0, at, 0))


def run_main(z, grad_scale, device, operands):
    rows = z.rows
    out_shape = []
    for index in range(len(SPANS)):
        out_shape += [shape_of((BLOCKS // 2, z.piece_rows(index), LANES))] * 2
    rows_shape = [
        shape_of((z.experts, rows, z.out), bf16),
        shape_of((z.experts, rows, z.hidden), bf16),
        shape_of((rows, LANES)),
        shape_of((rows, LANES), bf16),
    ]
    out_shape += rows_shape
    scratch = [pltpu.VMEM(v.shape, v.dtype) for v in operands]
    scratch += [pltpu.SemaphoreType.DMA((len(operands),))]
    scratch += [pltpu.SemaphoreType.DMA((4 * z.experts + 4,))]
    scratch += [pltpu.VMEM((rows, z.d_in), bf16)]
    scratch += [pltpu.VMEM(v.shape, v.dtype) for v in rows_shape]
    scratch += [pltpu.VMEM((z.small_rows * BLOCKS, LANES), f32)]
    scratch += [
        pltpu.VMEM((BLOCKS, z.piece_rows(index), LANES), f32) for index in range(len(SPANS))
    ]
    macs = rows * z.experts * 3 * (z.d_in * z.hidden + z.hidden * z.out)
    return pl.pallas_call(
        functools.partial(main_kernel, z, grad_scale),
        in_specs=[SMEM] + [ANY] * len(operands),
        out_specs=[ANY] * len(out_shape),
        out_shape=out_shape,
        scratch_shapes=scratch,
        compiler_params=pltpu.CompilerParams(vmem_limit_bytes=54 * MIB),
        cost_estimate=pl.CostEstimate(
            flops=2 * macs,
            bytes_accessed=20 * MIB,
            transcendentals=rows * z.experts * z.hidden,
        ),
        name="experts",
    )(device, *operands)


def run_outputs(z, weights, logit_grad, w_first, gain, bias, gates, normed, firsts):
    block = z.rows // 4
    out_shape = [shape_of((z.tasks + 1, z.rows, z.out), bf16), shape_of((z.rows, z.dense))]
    return pl.pallas_call(
        functools.partial(outputs_kernel, z),
        grid=(z.rows // block,),
        in_specs=[rows_spec(z, block, v.shape) for v in (weights, logit_grad)]
        + [whole(v) for v in (w_first, gain, bias) + gates]
        + [rows_spec(z, block, v.shape) for v in (normed, firsts)],
        out_specs=[rows_spec(z, block, v.shape) for v in out_shape],
        out_shape=out_shape,
        compiler_params=pltpu.CompilerParams(vmem_limit_bytes=24 * MIB),
        cost_estimate=pl.CostEstimate(
            flops=2 * z.rows * z.experts * z.hidden * z.dense,
            bytes_accessed=11 * MIB,
            transcendentals=0,
        ),
        name="outputs",
    )(weights, logit_grad, w_first, gain, bias, *gates, normed, firsts)


def run_unpack(z, index, device, near, far, earlier):
    last = index == len(SPANS) - 1
    lo, hi = SPANS[index]
    out_shape = [
        shape_of((z.experts, z.d_in, z.hidden)),
        shape_of((z.experts, z.hidden, z.out)),
    ]
    out_specs = [pl.BlockSpec((1,) + v.shape[1:], lambda at: (lo + at, 0, 0)) for v in out_shape]
    scratch = []
    if last:
        small = [
            shape_of((z.emb, z.vocab)),
            shape_of((z.tasks, z.gate, z.d_in)),
            shape_of((z.tasks, z.gate)),
            shape_of((z.experts, z.d_in)),
            shape_of((1, z.experts)),
        ] + [shape_of((z.experts, z.out))] * 4
        out_shape += small
        out_specs += [whole(v) for v in small]
        scratch = [pltpu.VMEM((z.small_rows * BLOCKS, LANES), f32)]
    operands = [device, near, far] + list(earlier)
    return pl.pallas_call(
        functools.partial(unpack_kernel, z, index),
        grid=(hi - lo,),
        in_specs=[SMEM, whole(near), whole(far)] + [ANY] * len(earlier),
        out_specs=out_specs,
        out_shape=out_shape,
        scratch_shapes=scratch,
        input_output_aliases={3: 0, 4: 1} if earlier else {},
        compiler_params=pltpu.CompilerParams(vmem_limit_bytes=24 * MIB),
        cost_estimate=pl.CostEstimate(flops=0, bytes_accessed=4 * MIB, transcendentals=0),
        name="unpack_%d" % index,
    )(*operands)


def exchange(value, axis):
    flip = FLIPS[axis]
    count = lax.axis_size("wide") * lax.axis_size("narrow")
    return lax.ppermute(value, BOTH, [(i, i ^ flip) for i in range(count)])


def after(value, other):
    return lax.optimization_barrier((value, other))[0]


def sum_pieces(near, far, outputs):
    count = len(near)
    got = [exchange(v, "c") for v in far]
    sent = None
    for step in range(HALVED):
        for i in range(count):
            found = got[i] if sent is None else after(got[i], sent)
            half = near[i].shape[0] // 2
            low, high = near[i][:half] + found[:half], near[i][half:] + found[half:]
            near[i] = low
            got[i] = exchange(high, ORDERS[i][step])
            sent = high
    for i in range(count):
        near[i] = near[i] + after(got[i], sent)
    rows = [v.shape[1] for v in near]
    joined = jnp.concatenate(near, axis=1)
    results = outputs(joined)
    joined = joined + after(exchange(joined, "2"), results[0])
    near = []
    for i in range(count):
        near.append(joined[:, sum(rows[:i]) : sum(rows[: i + 1])])
    for step in reversed(range(HALVED)):
        for i in range(count):
            if step < HALVED - 1:
                near[i] = jnp.concatenate([near[i], after(got[i], sent)], axis=0)
            got[i] = exchange(near[i], ORDERS[i][step])
            sent = near[i]
    far = []
    for i in range(count):
        near[i] = jnp.concatenate([near[i], after(got[i], sent)], axis=0)
        sent = near[i]
        far.append(exchange(near[i], "c"))
    return near, far, results


def local(
    fits,
    dense_feats,
    sparse_ids,
    presence,
    embed_table,
    w_first,
    b_first,
    w_second,
    b_second,
    ln_gain,
    ln_bias,
    gate_task,
    gate_task_bias,
    gate_shared,
    gate_shared_bias,
    cotangent,
):
    z = Sizes(dense_feats, sparse_ids, embed_table, w_first, w_second, gate_task)
    total_rows = z.rows * lax.axis_size("wide") * lax.axis_size("narrow")
    grad_scale = 1.0 / math.sqrt(total_rows)
    if fits:
        device = lax.axis_index("wide") * lax.axis_size("narrow") + lax.axis_index("narrow")
    else:
        device = 0
    device = jnp.full((1,), device, jnp.int32)
    ids, present = sparse_ids.T, presence.T
    gates = (gate_task.transpose(0, 2, 1), gate_shared.T)
    found = run_main(
        z,
        grad_scale,
        device,
        [
            ids,
            present,
            embed_table.T,
            gates[0],
            gate_task_bias,
            gates[1],
            gate_shared_bias.reshape(1, -1),
            dense_feats,
            w_first,
            b_first,
            w_second,
            b_second,
            ln_gain,
            ln_bias,
            cotangent,
        ],
    )
    near, far = list(found[: 2 * len(SPANS) : 2]), list(found[1 : 2 * len(SPANS) : 2])
    normed, firsts, weights, logit_grad = found[2 * len(SPANS) :]

    def outputs(begin):
        first = weights if begin is None else after(weights, begin)
        return run_outputs(
            z, first, logit_grad, w_first, ln_gain, ln_bias, gates, normed, firsts
        )

    if fits:
        near, far, results = sum_pieces(near, far, outputs)
    else:
        results = outputs(None)
        near, far = lax.psum((near, far), BOTH)
    mixed, dense_grad = results
    grads = ()
    for index in range(len(SPANS)):
        grads = run_unpack(z, index, device, near[index], far[index], grads[:2])
    w_first_grad, w_second_grad, table_grad = grads[:3]
    gate_task_grad, gate_task_bias_grad, gate_shared_grad, gate_shared_bias_grad = grads[3:7]
    b_first_grad, b_second_grad, gain_grad, bias_grad = grads[7:]
    return (
        mixed,
        dense_grad,
        table_grad.T,
        w_first_grad,
        b_first_grad,
        w_second_grad,
        b_second_grad,
        gain_grad,
        bias_grad,
        gate_task_grad.transpose(0, 2, 1),
        gate_task_bias_grad,
        gate_shared_grad.T,
        gate_shared_bias_grad.reshape(-1),
    )


def solution(mesh):
    fits = (mesh.shape["wide"], mesh.shape["narrow"]) == (8, 4)
    rows = P(BOTH, None)
    middle = P(None, BOTH, None)
    return jax.shard_map(
        functools.partial(local, fits),
        mesh=mesh,
        in_specs=(rows, rows, rows) + (P(),) * 11 + (middle,),
        out_specs=(middle, rows) + (P(),) * 11,
        check_vma=False,
    )
```

```python
import functools
import math

import jax
import jax.numpy as jnp
from jax import lax
from jax.experimental import pallas as pl
from jax.experimental.pallas import tpu as pltpu
from jax.sharding import PartitionSpec as P

f32 = jnp.float32
bf16 = jnp.bfloat16
epsilon = 1e-05
LANES = 128
DEVICES = 32
MIB = 1 << 20
LAG = 2
BOTH = ("wide", "narrow")
SPANS = ((0, 2), (2, 4), (4, 6))
FLIPS = {"c": 1, "x": 2, "y": 4, "1": 8, "2": 16}
AXES = "xy1"
ORDERS = ("xy1", "y1x", "1xy")
HALVED = len(AXES)
BLOCKS = 2 << HALVED


def dot(a, b):
    return lax.dot_general(a, b, (((1,), (0,)), ((), ())), preferred_element_type=f32)


def dot_nt(a, b):
    return lax.dot_general(a, b, (((1,), (1,)), ((), ())), preferred_element_type=f32)


def dot_tn(a, b):
    return lax.dot_general(a, b, (((0,), (0,)), ((), ())), preferred_element_type=f32)


def iota(shape, axis):
    return lax.broadcasted_iota(jnp.int32, shape, axis)


def ones_where(condition):
    return jnp.where(condition, 1.0, 0.0).astype(bf16)


class Sizes:
    def __init__(self, dense, ids, table, w_first, w_second, gate_task):
        self.rows, self.dense = dense.shape
        self.fields = ids.shape[1]
        self.vocab, self.emb = table.shape
        self.experts, self.d_in, self.hidden = w_first.shape
        self.out = w_second.shape[2]
        self.tasks, _, self.gate = gate_task.shape
        self.spec = (self.experts - self.gate) // (self.tasks - 1)
        self.low = LANES // self.emb
        self.high = self.vocab // self.low
        self.columns = gate_columns(self.experts, self.tasks, self.spec)
        self.width = self.tasks * self.gate + self.experts
        self.first_rows = self.d_in // BLOCKS
        self.second_rows = self.hidden // BLOCKS
        self.halves = self.out // LANES
        self.expert_rows = (self.first_rows + self.second_rows) * self.halves
        self.sum_rows = 4 * self.halves
        self.gate_rows = 16 * (self.d_in // LANES)
        self.gate_at = self.high
        self.sums_at = self.gate_at + self.gate_rows
        self.bias_at = self.sums_at + self.experts * self.sum_rows
        self.small_rows = -(-(self.bias_at + 1) // (8 * BLOCKS)) * 8

    def piece_rows(self, index):
        lo, hi = SPANS[index]
        last = index == len(SPANS) - 1
        return (hi - lo) * self.expert_rows + (self.small_rows if last else 0)


def gate_columns(experts, tasks, spec):
    shared = tasks * spec
    gate = spec + experts - shared
    columns = []
    for e in range(experts):
        found = []
        for k in range(tasks):
            if e >= shared:
                found.append((k, k * gate + spec + e - shared))
            elif e // spec == k:
                found.append((k, k * gate + e - k * spec))
        found.append((tasks, tasks * gate + e))
        columns.append(found)
    return columns


def gate_matrix(z, gate_task_ref, gate_shared_ref):
    total = None
    for k in range(z.tasks + 1):
        mat = gate_task_ref[k] if k < z.tasks else gate_shared_ref[...]
        n = mat.shape[0]
        place = ones_where(iota((LANES, n), 0) == iota((LANES, n), 1) + k * z.gate)
        part = dot(place, mat)
        total = part if total is None else total + part
    return total.astype(bf16)


def gate_bias(z, task_ref, shared_ref):
    total = None
    for k in range(z.tasks + 1):
        row = task_ref[k : k + 1, :] if k < z.tasks else shared_ref[...]
        n = row.shape[1]
        place = ones_where(iota((n, LANES), 1) == iota((n, LANES), 0) + k * z.gate)
        part = dot(row, place)
        total = part if total is None else total + part
    return total


def gate_lanes(z, k, shape):
    lane = iota(shape, 1)
    first = k * z.gate
    last = first + (z.gate if k < z.tasks else z.experts)
    return (lane >= first) & (lane < last)


def spread_matrix(z, f):
    a = iota((LANES, LANES), 0)
    b = iota((LANES, LANES), 1)
    return ones_where(b == f * z.emb + lax.rem(a, z.emb))


def table_block(z, table_ref):
    return jnp.concatenate(
        [table_ref[:, low * z.high : (low + 1) * z.high] for low in range(z.low)], axis=0
    )


def split_ids(z, ids_ref, presence_ref):
    ids = ids_ref[...]
    row = jnp.where(presence_ref[...] > 0, lax.bitwise_and(ids, z.high - 1), -1)
    return row, lax.div(ids, z.high)


def turned(v):
    return v.astype(f32).T.astype(jnp.int32)


def lookup_part(z, block, spreads, ids_ref, presence_ref):
    row, low = split_ids(z, ids_ref, presence_ref)
    row, low = turned(row), turned(low)
    lane_high = iota((z.rows, z.high), 1)
    lane_low = lax.div(iota((z.rows, LANES), 1), z.emb)
    total = None
    for f in range(z.fields):
        found = dot_nt(ones_where(row[:, f : f + 1] == lane_high), block)
        kept = jnp.where(low[:, f : f + 1] == lane_low, found, 0.0).astype(bf16)
        part = dot(kept, spreads[f])
        total = part if total is None else total + part
    return total


def softmax_part(z, logits):
    result = None
    for k in range(z.tasks + 1):
        lanes = gate_lanes(z, k, logits.shape)
        top = jnp.max(jnp.where(lanes, logits, -jnp.inf), axis=1, keepdims=True)
        value = jnp.exp(jnp.where(lanes, logits - top, -jnp.inf))
        value = value / jnp.sum(value, axis=1, keepdims=True)
        result = value if result is None else result + value
    return result


def logit_part(z, weights, along):
    product = weights * along
    total = jnp.zeros_like(product)
    for k in range(z.tasks + 1):
        lanes = gate_lanes(z, k, product.shape)
        found = jnp.sum(jnp.where(lanes, product, 0.0), axis=1, keepdims=True)
        total = jnp.where(lanes, found, total)
    return (weights * (along - total)).astype(bf16)


def table_part(z, embed, spreads, ids_ref, presence_ref):
    row, low = split_ids(z, ids_ref, presence_ref)
    low = turned(low)
    line_high = iota((z.high, z.rows), 0)
    lane_low = lax.div(iota((z.rows, LANES), 1), z.emb)
    hots = []
    kept = []
    for f in range(z.fields):
        hots.append(ones_where(row[f : f + 1, :] == line_high))
        wide = dot_nt(embed, spreads[f])
        kept.append(jnp.where(low[:, f : f + 1] == lane_low, wide, 0.0).astype(bf16))
    return dot(jnp.concatenate(hots, axis=1), jnp.concatenate(kept, axis=0))


def device_bits(device):
    own = jnp.int32(0)
    for axis in AXES:
        own = own * 2 + lax.bitwise_and(lax.div(device, FLIPS[axis]), 1)
    return lax.bitwise_and(device, 1), own


def block_of(shard, order, core, own):
    count = BLOCKS // 2
    flips = lax.bitwise_xor(own, shard % count)
    q = jnp.int32(0)
    for axis in order:
        bit = lax.bitwise_and(lax.shift_right_logical(flips, HALVED - 1 - AXES.index(axis)), 1)
        q = q * 2 + bit
    return lax.bitwise_xor(core, shard // count) * count + q


def column_matrix(z, k, ref):
    total = None
    row = iota((LANES, z.out), 0)
    for e in range(z.experts):
        for gate, column in z.columns[e]:
            if gate == k:
                part = jnp.where(row == column, ref[e : e + 1, :].astype(f32), 0.0)
                total = part if total is None else total + part
    return total.astype(bf16)


def main_kernel(z, grad_scale, *refs):
    refs = list(refs)

    def take(count):
        return [refs.pop(0) for _ in range(count)]

    (device_ref,) = take(1)
    far_refs = take(15)
    piece_refs = [take(2) for _ in SPANS]
    normed_ref, first_ref, weights_ref, logit_ref = take(4)
    here = take(15)
    sems, out_sems, features_s, normed_s, first_s, weights_s, logit_s, small_s = take(8)
    packed_s = take(len(SPANS))
    copies = [
        pltpu.make_async_copy(a, b, sems.at[i]) for i, (a, b) in enumerate(zip(far_refs, here))
    ]
    for copy in copies:
        copy.start()
    sent = []

    def send(source, target):
        copy = pltpu.make_async_copy(source, target, out_sems.at[len(sent)])
        copy.start()
        sent.append(copy)

    core, own = device_bits(device_ref[0])
    ids_ref, presence_ref, table_ref, gate_task_ref, gate_task_bias_ref = here[:5]
    gate_shared_ref, gate_shared_bias_ref, dense_ref, w_first_ref, b_first_ref = here[5:10]
    w_second_ref, b_second_ref, gain_ref, bias_ref, cot_ref = here[10:]
    spreads = [spread_matrix(z, f) for f in range(z.fields)]
    for copy in copies[:3]:
        copy.wait()
    looked = lookup_part(z, table_block(z, table_ref), spreads, ids_ref, presence_ref)
    features_s[:, z.dense :] = (0.5 * looked).astype(bf16)
    for copy in copies[3:8]:
        copy.wait()
    features_s[:, : z.dense] = dense_ref[...] * 0.5
    gates = gate_matrix(z, gate_task_ref, gate_shared_ref)
    features = features_s[...]
    logits = 2.0 * dot_nt(features, gates)
    weights = softmax_part(z, logits + gate_bias(z, gate_task_bias_ref, gate_shared_bias_ref))
    weights_s[...] = weights
    send(weights_s, weights_ref)
    for copy in copies[8:]:
        copy.wait()
    lane = iota((z.rows, LANES), 1)
    along = None
    few = weights.astype(bf16)
    bias_sums = []
    for k in range(z.tasks + 1):
        part = dot_nt(cot_ref[k], column_matrix(z, k, bias_ref))
        along = part if along is None else along + part
        bias_sums.append(dot_tn(few, cot_ref[k]))
    held = {"along": along, "embed": jnp.zeros((z.rows, LANES), f32)}
    scale = 1.0 / z.out

    def expert(index, e):
        span = SPANS[index]

        def row(ref):
            return ref[e : e + 1, :].astype(f32)

        def mean(v):
            return jnp.sum(v, axis=1, keepdims=True) * scale

        def keep(q, v):
            for h in range(z.halves):
                line = z.sums_at + e * z.sum_rows + q * z.halves + h
                small_s[line : line + 1, :] = v[:, h * LANES : (h + 1) * LANES]

        def total(v):
            return jnp.sum(v, axis=0, keepdims=True)

        gain = row(gain_ref)
        half = dot(features_s[...], w_first_ref[e]) + 0.5 * row(b_first_ref)
        yield
        turn = jnp.tanh(half)
        up = 1.0 + turn
        smooth = half * up
        hidden = smooth.astype(bf16)
        yield
        second = dot(hidden, w_second_ref[e]) + row(b_second_ref)
        yield
        center = second - mean(second)
        inverse = lax.rsqrt(mean(center * center) + epsilon)
        normed = center * inverse
        normed_s[e] = normed.astype(bf16)
        send(normed_s.at[e], normed_ref.at[e])
        low = normed.astype(bf16)
        low_gain = gain_ref[e : e + 1, :]
        gained = low * low_gain
        upstream = None
        along = held["along"]
        for k, column in z.columns[e]:
            cot = cot_ref[k]
            part = few[:, column : column + 1] * cot
            upstream = part if upstream is None else upstream + part
            found = jnp.sum((cot * gained).astype(f32), axis=1, keepdims=True)
            along = jnp.where(lane == column, along + found, along)
        held["along"] = along
        product = upstream * low
        scaled = upstream * low_gain
        average = jnp.full((z.out, LANES), scale, bf16)
        first_mean = dot(scaled, average).astype(bf16)
        second_mean = dot(product * low_gain, average).astype(bf16)
        first_mean = jnp.concatenate([first_mean] * z.halves, axis=1)
        second_mean = jnp.concatenate([second_mean] * z.halves, axis=1)
        second_grad = inverse.astype(bf16) * (scaled - first_mean - low * second_mean)
        ones = jnp.ones((16, z.rows), bf16)
        keep(1, dot(ones, second_grad)[:1])
        keep(2, dot(ones, product)[:1])
        yield
        hidden_grad = dot_nt(second_grad, w_second_ref[e])
        second_total = dot_tn(hidden, second_grad) * grad_scale
        yield
        first_grad = hidden_grad * (up + smooth * (1.0 - turn))
        keep(0, 0.5 * total(first_grad))
        first_s[e] = first_grad.astype(bf16)
        send(first_s.at[e], first_ref.at[e])
        yield
        first_total = dot_tn(features_s[...], first_s[e]) * grad_scale
        held["embed"] = held["embed"] + dot_nt(first_s[e], w_first_ref[e, z.dense :, :])
        found = None
        for k, column in z.columns[e]:
            part = bias_sums[k][column : column + 1, :]
            found = part if found is None else found + part
        keep(3, found)
        line = (e - span[0]) * z.expert_rows
        lines = pl.ds(line, z.expert_rows)
        for shard in range(BLOCKS):
            at = block_of(shard, ORDERS[index], core, own)
            begin = line
            for v, count in ((first_total, z.first_rows), (second_total, z.second_rows)):
                for h in range(z.halves):
                    packed_s[index][at, begin : begin + count, :] = v[
                        shard * count : (shard + 1) * count, h * LANES : (h + 1) * LANES
                    ]
                    begin += count
        for side in range(2):
            blocks = pl.ds(side * (BLOCKS // 2), BLOCKS // 2)
            send(packed_s[index].at[blocks, lines, :], piece_refs[index][side].at[:, lines, :])
        yield

    chains = [expert(index, e) for index, span in enumerate(SPANS) for e in range(*span)]
    for _ in range(3):
        next(chains[0])
    for this, then in zip(chains, chains[1:] + [iter([None] * 7)]):
        next(then)
        next(this)
        next(this)
        next(then)
        next(then)
        next(this)
        next(this)
    along, embed = held["along"], held["embed"]
    logit_grad = logit_part(z, weights_s[...], along)
    logit_s[...] = logit_grad
    send(logit_s, logit_ref)
    gate_total = 2.0 * dot_tn(logit_grad, features_s[...])
    embed = 0.5 * embed + dot(logit_grad, gates[:, z.dense :])
    table_total = table_part(z, embed.astype(bf16), spreads, ids_ref, presence_ref)
    small_s[: z.high, :] = table_total.T
    for q in range(z.d_in // LANES):
        line = z.gate_at + q * 16
        small_s[line : line + 16, :] = gate_total[:16, q * LANES : (q + 1) * LANES]
    small_s[z.bias_at :, :] = jnp.zeros_like(small_s[z.bias_at :, :])
    small_s[z.bias_at : z.bias_at + 1, :] = jnp.sum(logit_grad.astype(f32), axis=0, keepdims=True)
    lines = pl.ds((SPANS[-1][1] - SPANS[-1][0]) * z.expert_rows, z.small_rows)
    for shard in range(BLOCKS):
        at = block_of(shard, ORDERS[-1], core, own)
        packed_s[-1][at, lines, :] = (
            small_s[shard * z.small_rows : (shard + 1) * z.small_rows, :] * grad_scale
        )
    for side in range(2):
        blocks = pl.ds(side * (BLOCKS // 2), BLOCKS // 2)
        send(packed_s[-1].at[blocks, lines, :], piece_refs[-1][side].at[:, lines, :])
    for copy in sent:
        copy.wait()


def outputs_kernel(z, *refs):
    weights_ref, logit_ref, w_first_ref, gain_ref, bias_ref, gate_task_ref, gate_shared_ref = refs[
        :7
    ]
    normed_ref, first_ref, mixed_ref, dense_ref = refs[7:]
    weights = weights_ref[...]
    mixed = [None] * (z.tasks + 1)
    gates = gate_matrix(z, gate_task_ref, gate_shared_ref)
    dense = None
    for e in range(z.experts):
        expert_out = normed_ref[e].astype(f32) * gain_ref[e : e + 1, :].astype(f32) + bias_ref[
            e : e + 1, :
        ].astype(f32)
        for k, column in z.columns[e]:
            part = weights[:, column : column + 1] * expert_out
            mixed[k] = part if mixed[k] is None else mixed[k] + part
        part = dot_nt(first_ref[e], w_first_ref[e, : z.dense, :])
        dense = part if dense is None else dense + part
    for k in range(z.tasks + 1):
        mixed_ref[k] = mixed[k].astype(bf16)
    dense_ref[...] = 0.5 * dense + dot(logit_ref[...], gates[:, : z.dense])


def unpack_kernel(z, index, side, place_ref, device_ref, piece_ref, *refs):
    last = index == len(SPANS) - 1 and side == 1
    refs = list(refs)

    def take(count):
        return [refs.pop(0) for _ in range(count)]

    if last:
        small_refs = take(2)
    if index or side:
        take(2)
    w_first_ref, w_second_ref = take(2)
    core, own = device_bits(device_ref[0])
    count = BLOCKS // 2

    def at(shard):
        return lax.bitwise_and(block_of(shard, ORDERS[index], core, own), count - 1)

    for shard in range(count):
        block = at(shard)
        line = 0
        for ref, rows in ((w_first_ref, z.first_rows), (w_second_ref, z.second_rows)):
            for h in range(z.halves):
                ref[0, shard * rows : (shard + 1) * rows, h * LANES : (h + 1) * LANES] = (
                    piece_ref[block, line : line + rows, :]
                )
                line += rows
    if not last:
        return
    table_ref, gate_task_ref, gate_task_bias_ref, gate_shared_ref, gate_shared_bias_ref = take(5)
    sum_refs = take(4)
    (small_s,) = take(1)

    @pl.when(pl.program_id(0) == 0)
    def _():
        for half, from_ref in enumerate(small_refs):
            start = lax.bitwise_xor(core, half) * (count * z.small_rows)
            for shard in range(count):
                lines = pl.ds(pl.multiple_of(start + shard * z.small_rows, 8), z.small_rows)
                small_s[lines, :] = from_ref[at(shard)]
        for low in range(z.low):
            table_ref[:, low * z.high : (low + 1) * z.high] = small_s[
                low * z.emb : (low + 1) * z.emb, :
            ]
        for q in range(z.d_in // LANES):
            line = z.gate_at + q * 16
            lanes = slice(q * LANES, (q + 1) * LANES)
            for k in range(z.tasks):
                gate_task_ref[k, :, lanes] = small_s[
                    line + k * z.gate : line + (k + 1) * z.gate, :
                ]
            gate_shared_ref[:, lanes] = small_s[line + z.tasks * z.gate : line + z.width, :]
        bias_row = small_s[z.bias_at : z.bias_at + 1, :]
        for k in range(z.tasks):
            gate_task_bias_ref[k : k + 1, :] = bias_row[:, k * z.gate : (k + 1) * z.gate]
        gate_shared_bias_ref[...] = bias_row[:, z.tasks * z.gate : z.width]
        for e in range(z.experts):
            for q in range(4):
                for h in range(z.halves):
                    line = z.sums_at + e * z.sum_rows + q * z.halves + h
                    sum_refs[q][e : e + 1, h * LANES : (h + 1) * LANES] = small_s[
                        line : line + 1, :
                    ]


SMEM = pl.BlockSpec(memory_space=pltpu.SMEM)
ANY = pl.BlockSpec(memory_space=pl.ANY)
HBM = pl.BlockSpec(memory_space=pltpu.HBM)


def shape_of(shape, dtype=f32):
    return jax.ShapeDtypeStruct(shape, dtype)


def whole(array):
    return pl.BlockSpec(array.shape, lambda at: (0,) * len(array.shape))


def rows_spec(z, block, shape):
    if shape == (z.fields, z.rows):
        return pl.BlockSpec((z.fields, block), lambda at: (0, at))
    if len(shape) == 2:
        return pl.BlockSpec((block, shape[1]), lambda at: (at, 0))
    return pl.BlockSpec((shape[0], block, shape[2]), lambda at: (0, at, 0))


def run_main(z, grad_scale, device, operands):
    rows = z.rows
    out_shape = []
    for index in range(len(SPANS)):
        out_shape += [shape_of((BLOCKS // 2, z.piece_rows(index), LANES))] * 2
    rows_shape = [
        shape_of((z.experts, rows, z.out), bf16),
        shape_of((z.experts, rows, z.hidden), bf16),
        shape_of((rows, LANES)),
        shape_of((rows, LANES), bf16),
    ]
    out_shape += rows_shape
    scratch = [pltpu.VMEM(v.shape, v.dtype) for v in operands]
    scratch += [pltpu.SemaphoreType.DMA((len(operands),))]
    scratch += [pltpu.SemaphoreType.DMA((4 * z.experts + 4,))]
    scratch += [pltpu.VMEM((rows, z.d_in), bf16)]
    scratch += [pltpu.VMEM(v.shape, v.dtype) for v in rows_shape]
    scratch += [pltpu.VMEM((z.small_rows * BLOCKS, LANES), f32)]
    scratch += [
        pltpu.VMEM((BLOCKS, z.piece_rows(index), LANES), f32) for index in range(len(SPANS))
    ]
    macs = rows * z.experts * 3 * (z.d_in * z.hidden + z.hidden * z.out)
    return pl.pallas_call(
        functools.partial(main_kernel, z, grad_scale),
        in_specs=[SMEM] + [ANY] * len(operands),
        out_specs=[ANY] * len(out_shape),
        out_shape=out_shape,
        scratch_shapes=scratch,
        compiler_params=pltpu.CompilerParams(vmem_limit_bytes=54 * MIB),
        cost_estimate=pl.CostEstimate(
            flops=2 * macs,
            bytes_accessed=20 * MIB,
            transcendentals=rows * z.experts * z.hidden,
        ),
        name="experts",
    )(device, *operands)


def run_outputs(z, weights, logit_grad, w_first, gain, bias, gates, normed, firsts):
    block = z.rows // 4
    out_shape = [shape_of((z.tasks + 1, z.rows, z.out), bf16), shape_of((z.rows, z.dense))]
    return pl.pallas_call(
        functools.partial(outputs_kernel, z),
        grid=(z.rows // block,),
        in_specs=[rows_spec(z, block, v.shape) for v in (weights, logit_grad)]
        + [whole(v) for v in (w_first, gain, bias) + gates]
        + [rows_spec(z, block, v.shape) for v in (normed, firsts)],
        out_specs=[rows_spec(z, block, v.shape) for v in out_shape],
        out_shape=out_shape,
        compiler_params=pltpu.CompilerParams(vmem_limit_bytes=24 * MIB),
        cost_estimate=pl.CostEstimate(
            flops=2 * z.rows * z.experts * z.hidden * z.dense,
            bytes_accessed=11 * MIB,
            transcendentals=0,
        ),
        name="outputs",
    )(weights, logit_grad, w_first, gain, bias, *gates, normed, firsts)


def run_unpack(z, index, side, device, pieces, earlier):
    last = index == len(SPANS) - 1 and side == 1
    lo, hi = SPANS[index]
    half = BLOCKS // 2
    out_shape = [
        shape_of((z.experts, z.d_in, z.hidden)),
        shape_of((z.experts, z.hidden, z.out)),
    ]

    def half_spec(array):
        shape = (1, array.shape[1] // 2, array.shape[2])
        return pl.BlockSpec(shape, lambda at, place: (lo + at, lax.bitwise_xor(place[0], side), 0))

    def fixed(array):
        return pl.BlockSpec(array.shape, lambda at, place: (0,) * len(array.shape))

    out_specs = [half_spec(v) for v in out_shape]
    operands = [pieces[side]]
    in_specs = [SMEM, pl.BlockSpec((half, z.expert_rows, LANES), lambda at, place: (0, at, 0))]
    scratch = []
    if last:
        start = (hi - lo) * z.expert_rows // z.small_rows
        operands += list(pieces)
        in_specs += [
            pl.BlockSpec((half, z.small_rows, LANES), lambda at, place: (0, start, 0))
        ] * 2
    aliases = {2 + len(operands): 0, 3 + len(operands): 1} if earlier else {}
    operands += list(earlier)
    in_specs += [ANY] * len(earlier)
    if last:
        small = [
            shape_of((z.emb, z.vocab)),
            shape_of((z.tasks, z.gate, z.d_in)),
            shape_of((z.tasks, z.gate)),
            shape_of((z.experts, z.d_in)),
            shape_of((1, z.experts)),
        ] + [shape_of((z.experts, z.out))] * 4
        out_shape += small
        out_specs += [fixed(v) for v in small]
        scratch = [pltpu.VMEM((z.small_rows * BLOCKS, LANES), f32)]
    core = lax.bitwise_and(device, 1)
    return pl.pallas_call(
        functools.partial(unpack_kernel, z, index, side),
        grid_spec=pltpu.PrefetchScalarGridSpec(
            num_scalar_prefetch=1,
            grid=(hi - lo,),
            in_specs=in_specs,
            out_specs=out_specs,
            scratch_shapes=scratch,
        ),
        out_shape=out_shape,
        input_output_aliases=aliases,
        compiler_params=pltpu.CompilerParams(vmem_limit_bytes=24 * MIB),
        cost_estimate=pl.CostEstimate(flops=0, bytes_accessed=4 * MIB, transcendentals=0),
        name="unpack_%d_%d" % (index, side),
    )(core, device, *operands)


def exchange(value, axis):
    flip = FLIPS[axis]
    count = lax.axis_size("wide") * lax.axis_size("narrow")
    return lax.ppermute(value, BOTH, [(i, i ^ flip) for i in range(count)])


def after(value, other):
    return lax.optimization_barrier((value, other))[0]


def sum_pieces(near, far, outputs, unpack):
    count = len(near)
    got = [exchange(v, "c") for v in far]
    sent = None
    for step in range(HALVED):
        for i in range(count):
            found = got[i] if sent is None else after(got[i], sent)
            half = near[i].shape[0] // 2
            low, high = near[i][:half] + found[:half], near[i][half:] + found[half:]
            near[i] = low
            got[i] = exchange(high, ORDERS[i][step])
            sent = high
    for i in range(count):
        near[i] = near[i] + after(got[i], sent)
    rows = [v.shape[1] for v in near]
    joined = jnp.concatenate(near, axis=1)
    results = outputs(joined)
    joined = joined + after(exchange(joined, "2"), results[0])
    near = []
    for i in range(count):
        near.append(joined[:, sum(rows[:i]) : sum(rows[: i + 1])])
    for step in reversed(range(HALVED)):
        for i in range(count):
            if step < HALVED - 1:
                near[i] = jnp.concatenate([near[i], after(got[i], sent)], axis=0)
            got[i] = exchange(near[i], ORDERS[i][step])
            sent = near[i]
    far = []
    grads = ()
    for i in range(count):
        near[i] = jnp.concatenate([near[i], after(got[i], sent)], axis=0)
        if i:
            near[i] = after(near[i], grads[0])
        sent = near[i]
        far.append(exchange(near[i], "c"))
        grads = unpack(i, 0, near[i], None, grads)
    for i in range(count):
        grads = unpack(i, 1, near[i], far[i], grads)
    return grads, results


def local(
    fits,
    dense_feats,
    sparse_ids,
    presence,
    embed_table,
    w_first,
    b_first,
    w_second,
    b_second,
    ln_gain,
    ln_bias,
    gate_task,
    gate_task_bias,
    gate_shared,
    gate_shared_bias,
    cotangent,
):
    z = Sizes(dense_feats, sparse_ids, embed_table, w_first, w_second, gate_task)
    total_rows = z.rows * lax.axis_size("wide") * lax.axis_size("narrow")
    grad_scale = 1.0 / math.sqrt(total_rows)
    if fits:
        device = lax.axis_index("wide") * lax.axis_size("narrow") + lax.axis_index("narrow")
    else:
        device = 0
    device = jnp.full((1,), device, jnp.int32)
    ids, present = sparse_ids.T, presence.T
    gates = (gate_task.transpose(0, 2, 1), gate_shared.T)
    found = run_main(
        z,
        grad_scale,
        device,
        [
            ids,
            present,
            embed_table.T,
            gates[0],
            gate_task_bias,
            gates[1],
            gate_shared_bias.reshape(1, -1),
            dense_feats,
            w_first,
            b_first,
            w_second,
            b_second,
            ln_gain,
            ln_bias,
            cotangent,
        ],
    )
    near, far = list(found[: 2 * len(SPANS) : 2]), list(found[1 : 2 * len(SPANS) : 2])
    normed, firsts, weights, logit_grad = found[2 * len(SPANS) :]

    def outputs(begin):
        first = weights if begin is None else after(weights, begin)
        return run_outputs(
            z, first, logit_grad, w_first, ln_gain, ln_bias, gates, normed, firsts
        )

    def unpack(index, side, near, far, earlier):
        return run_unpack(z, index, side, device, (near, far), earlier)

    if fits:
        grads, results = sum_pieces(near, far, outputs, unpack)
    else:
        results = outputs(None)
        near, far = lax.psum((near, far), BOTH)
        grads = ()
        for side in range(2):
            for index in range(len(SPANS)):
                grads = unpack(index, side, near[index], far[index], grads)
    mixed, dense_grad = results
    w_first_grad, w_second_grad, table_grad = grads[:3]
    gate_task_grad, gate_task_bias_grad, gate_shared_grad, gate_shared_bias_grad = grads[3:7]
    b_first_grad, b_second_grad, gain_grad, bias_grad = grads[7:]
    return (
        mixed,
        dense_grad,
        table_grad.T,
        w_first_grad,
        b_first_grad,
        w_second_grad,
        b_second_grad,
        gain_grad,
        bias_grad,
        gate_task_grad.transpose(0, 2, 1),
        gate_task_bias_grad,
        gate_shared_grad.T,
        gate_shared_bias_grad.reshape(-1),
    )


def solution(mesh):
    fits = (mesh.shape["wide"], mesh.shape["narrow"]) == (8, 4)
    rows = P(BOTH, None)
    middle = P(None, BOTH, None)
    return jax.shard_map(
        functools.partial(local, fits),
        mesh=mesh,
        in_specs=(rows, rows, rows) + (P(),) * 11 + (middle,),
        out_specs=(middle, rows) + (P(),) * 11,
        check_vma=False,
    )
```

```python
import functools
import math

import jax
import jax.numpy as jnp
from jax import lax
from jax.experimental import pallas as pl
from jax.experimental.pallas import tpu as pltpu
from jax.sharding import PartitionSpec as P

f32 = jnp.float32
bf16 = jnp.bfloat16
epsilon = 1e-05
LANES = 128
DEVICES = 32
MIB = 1 << 20
LAG = 2
BOTH = ("wide", "narrow")
SPANS = ((0, 2), (2, 4), (4, 6))
FLIPS = {"c": 1, "x": 2, "y": 4, "1": 8, "2": 16}
ORDERS = ("xy12", "y1x2", "1xy2")
HALVED = 3
BLOCKS = 2 << HALVED


def dot(a, b):
    return lax.dot_general(a, b, (((1,), (0,)), ((), ())), preferred_element_type=f32)


def dot_nt(a, b):
    return lax.dot_general(a, b, (((1,), (1,)), ((), ())), preferred_element_type=f32)


def dot_tn(a, b):
    return lax.dot_general(a, b, (((0,), (0,)), ((), ())), preferred_element_type=f32)


def iota(shape, axis):
    return lax.broadcasted_iota(jnp.int32, shape, axis)


def ones_where(condition):
    return jnp.where(condition, 1.0, 0.0).astype(bf16)


class Sizes:
    def __init__(self, dense, ids, table, w_first, w_second, gate_task):
        self.rows, self.dense = dense.shape
        self.fields = ids.shape[1]
        self.vocab, self.emb = table.shape
        self.experts, self.d_in, self.hidden = w_first.shape
        self.out = w_second.shape[2]
        self.tasks, _, self.gate = gate_task.shape
        self.spec = (self.experts - self.gate) // (self.tasks - 1)
        self.low = LANES // self.emb
        self.high = self.vocab // self.low
        self.columns = gate_columns(self.experts, self.tasks, self.spec)
        self.width = self.tasks * self.gate + self.experts
        self.first_rows = self.d_in // BLOCKS
        self.second_rows = self.hidden // BLOCKS
        self.halves = self.out // LANES
        self.expert_rows = (self.first_rows + self.second_rows) * self.halves
        self.sum_rows = 4 * self.halves
        self.gate_rows = 16 * (self.d_in // LANES)
        self.gate_at = self.high
        self.sums_at = self.gate_at + self.gate_rows
        self.bias_at = self.sums_at + self.experts * self.sum_rows
        self.small_rows = -(-(self.bias_at + 1) // (8 * BLOCKS)) * 8

    def piece_rows(self, index):
        lo, hi = SPANS[index]
        last = index == len(SPANS) - 1
        return (hi - lo) * self.expert_rows + (self.small_rows if last else 0)


def gate_columns(experts, tasks, spec):
    shared = tasks * spec
    gate = spec + experts - shared
    columns = []
    for e in range(experts):
        found = []
        for k in range(tasks):
            if e >= shared:
                found.append((k, k * gate + spec + e - shared))
            elif e // spec == k:
                found.append((k, k * gate + e - k * spec))
        found.append((tasks, tasks * gate + e))
        columns.append(found)
    return columns


def gate_matrix(z, gate_task_ref, gate_shared_ref):
    total = None
    for k in range(z.tasks + 1):
        mat = gate_task_ref[k] if k < z.tasks else gate_shared_ref[...]
        n = mat.shape[0]
        place = ones_where(iota((LANES, n), 0) == iota((LANES, n), 1) + k * z.gate)
        part = dot(place, mat)
        total = part if total is None else total + part
    return total.astype(bf16)


def gate_bias(z, task_ref, shared_ref):
    total = None
    for k in range(z.tasks + 1):
        row = task_ref[k : k + 1, :] if k < z.tasks else shared_ref[...]
        n = row.shape[1]
        place = ones_where(iota((n, LANES), 1) == iota((n, LANES), 0) + k * z.gate)
        part = dot(row, place)
        total = part if total is None else total + part
    return total


def gate_lanes(z, k, shape):
    lane = iota(shape, 1)
    first = k * z.gate
    last = first + (z.gate if k < z.tasks else z.experts)
    return (lane >= first) & (lane < last)


def spread_matrix(z, f):
    a = iota((LANES, LANES), 0)
    b = iota((LANES, LANES), 1)
    return ones_where(b == f * z.emb + lax.rem(a, z.emb))


def table_block(z, table_ref):
    return jnp.concatenate(
        [table_ref[:, low * z.high : (low + 1) * z.high] for low in range(z.low)], axis=0
    )


def split_ids(z, ids_ref, presence_ref):
    ids = ids_ref[...]
    row = jnp.where(presence_ref[...] > 0, lax.bitwise_and(ids, z.high - 1), -1)
    return row, lax.div(ids, z.high)


def turned(v):
    return v.astype(f32).T.astype(jnp.int32)


def lookup_part(z, block, spreads, ids_ref, presence_ref):
    row, low = split_ids(z, ids_ref, presence_ref)
    row, low = turned(row), turned(low)
    lane_high = iota((z.rows, z.high), 1)
    lane_low = lax.div(iota((z.rows, LANES), 1), z.emb)
    total = None
    for f in range(z.fields):
        found = dot_nt(ones_where(row[:, f : f + 1] == lane_high), block)
        kept = jnp.where(low[:, f : f + 1] == lane_low, found, 0.0).astype(bf16)
        part = dot(kept, spreads[f])
        total = part if total is None else total + part
    return total


def softmax_part(z, logits):
    result = None
    for k in range(z.tasks + 1):
        lanes = gate_lanes(z, k, logits.shape)
        top = jnp.max(jnp.where(lanes, logits, -jnp.inf), axis=1, keepdims=True)
        value = jnp.exp(jnp.where(lanes, logits - top, -jnp.inf))
        value = value / jnp.sum(value, axis=1, keepdims=True)
        result = value if result is None else result + value
    return result


def logit_part(z, weights, along):
    product = weights * along
    total = jnp.zeros_like(product)
    for k in range(z.tasks + 1):
        lanes = gate_lanes(z, k, product.shape)
        found = jnp.sum(jnp.where(lanes, product, 0.0), axis=1, keepdims=True)
        total = jnp.where(lanes, found, total)
    return (weights * (along - total)).astype(bf16)


def table_part(z, embed, spreads, ids_ref, presence_ref):
    row, low = split_ids(z, ids_ref, presence_ref)
    low = turned(low)
    line_high = iota((z.high, z.rows), 0)
    lane_low = lax.div(iota((z.rows, LANES), 1), z.emb)
    hots = []
    kept = []
    for f in range(z.fields):
        hots.append(ones_where(row[f : f + 1, :] == line_high))
        wide = dot_nt(embed, spreads[f])
        kept.append(jnp.where(low[:, f : f + 1] == lane_low, wide, 0.0).astype(bf16))
    return dot(jnp.concatenate(hots, axis=1), jnp.concatenate(kept, axis=0))


def device_bits(device, order):
    own = jnp.int32(0)
    for axis in order[:HALVED]:
        own = own * 2 + lax.bitwise_and(lax.div(device, FLIPS[axis]), 1)
    return lax.bitwise_and(device, 1), own


def block_of(shard, core, own):
    count = BLOCKS // 2
    return lax.bitwise_xor(core, shard // count) * count + lax.bitwise_xor(own, shard % count)


def column_matrix(z, k, ref):
    total = None
    row = iota((LANES, z.out), 0)
    for e in range(z.experts):
        for gate, column in z.columns[e]:
            if gate == k:
                part = jnp.where(row == column, ref[e : e + 1, :].astype(f32), 0.0)
                total = part if total is None else total + part
    return total.astype(bf16)


def main_kernel(z, grad_scale, *refs):
    refs = list(refs)

    def take(count):
        return [refs.pop(0) for _ in range(count)]

    (device_ref,) = take(1)
    far_refs = take(15)
    piece_refs = [take(2) for _ in SPANS]
    normed_ref, first_ref, weights_ref, logit_ref = take(4)
    here = take(15)
    sems, out_sems, features_s, normed_s, first_s, weights_s, logit_s, small_s = take(8)
    packed_s = take(len(SPANS))
    copies = [
        pltpu.make_async_copy(a, b, sems.at[i]) for i, (a, b) in enumerate(zip(far_refs, here))
    ]
    for copy in copies:
        copy.start()
    sent = []

    def send(source, target):
        copy = pltpu.make_async_copy(source, target, out_sems.at[len(sent)])
        copy.start()
        sent.append(copy)

    places = [device_bits(device_ref[0], order) for order in ORDERS]
    ids_ref, presence_ref, table_ref, gate_task_ref, gate_task_bias_ref = here[:5]
    gate_shared_ref, gate_shared_bias_ref, dense_ref, w_first_ref, b_first_ref = here[5:10]
    w_second_ref, b_second_ref, gain_ref, bias_ref, cot_ref = here[10:]
    spreads = [spread_matrix(z, f) for f in range(z.fields)]
    for copy in copies[:3]:
        copy.wait()
    looked = lookup_part(z, table_block(z, table_ref), spreads, ids_ref, presence_ref)
    features_s[:, z.dense :] = (0.5 * looked).astype(bf16)
    for copy in copies[3:8]:
        copy.wait()
    features_s[:, : z.dense] = dense_ref[...] * 0.5
    gates = gate_matrix(z, gate_task_ref, gate_shared_ref)
    features = features_s[...]
    logits = 2.0 * dot_nt(features, gates)
    weights = softmax_part(z, logits + gate_bias(z, gate_task_bias_ref, gate_shared_bias_ref))
    weights_s[...] = weights
    send(weights_s, weights_ref)
    for copy in copies[8:]:
        copy.wait()
    lane = iota((z.rows, LANES), 1)
    along = None
    few = weights.astype(bf16)
    bias_sums = []
    for k in range(z.tasks + 1):
        part = dot_nt(cot_ref[k], column_matrix(z, k, bias_ref))
        along = part if along is None else along + part
        bias_sums.append(dot_tn(few, cot_ref[k]))
    held = {"along": along, "embed": jnp.zeros((z.rows, LANES), f32)}
    scale = 1.0 / z.out

    def expert(index, e):
        span = SPANS[index]

        def row(ref):
            return ref[e : e + 1, :].astype(f32)

        def mean(v):
            return jnp.sum(v, axis=1, keepdims=True) * scale

        def keep(q, v):
            for h in range(z.halves):
                line = z.sums_at + e * z.sum_rows + q * z.halves + h
                small_s[line : line + 1, :] = v[:, h * LANES : (h + 1) * LANES]

        def total(v):
            return jnp.sum(v, axis=0, keepdims=True)

        gain = row(gain_ref)
        half = dot(features_s[...], w_first_ref[e]) + 0.5 * row(b_first_ref)
        yield
        turn = jnp.tanh(half)
        up = 1.0 + turn
        smooth = half * up
        hidden = smooth.astype(bf16)
        yield
        second = dot(hidden, w_second_ref[e]) + row(b_second_ref)
        yield
        center = second - mean(second)
        inverse = lax.rsqrt(mean(center * center) + epsilon)
        normed = center * inverse
        normed_s[e] = normed.astype(bf16)
        send(normed_s.at[e], normed_ref.at[e])
        low = normed.astype(bf16)
        low_gain = gain_ref[e : e + 1, :]
        gained = low * low_gain
        upstream = None
        along = held["along"]
        for k, column in z.columns[e]:
            cot = cot_ref[k]
            part = few[:, column : column + 1] * cot
            upstream = part if upstream is None else upstream + part
            found = jnp.sum((cot * gained).astype(f32), axis=1, keepdims=True)
            along = jnp.where(lane == column, along + found, along)
        held["along"] = along
        product = upstream * low
        scaled = upstream * low_gain
        average = jnp.full((z.out, LANES), scale, bf16)
        first_mean = dot(scaled, average).astype(bf16)
        second_mean = dot(product * low_gain, average).astype(bf16)
        first_mean = jnp.concatenate([first_mean] * z.halves, axis=1)
        second_mean = jnp.concatenate([second_mean] * z.halves, axis=1)
        second_grad = inverse.astype(bf16) * (scaled - first_mean - low * second_mean)
        ones = jnp.ones((16, z.rows), bf16)
        keep(1, dot(ones, second_grad)[:1])
        keep(2, dot(ones, product)[:1])
        yield
        hidden_grad = dot_nt(second_grad, w_second_ref[e])
        second_total = dot_tn(hidden, second_grad) * grad_scale
        yield
        first_grad = hidden_grad * (up + smooth * (1.0 - turn))
        keep(0, 0.5 * total(first_grad))
        first_s[e] = first_grad.astype(bf16)
        send(first_s.at[e], first_ref.at[e])
        yield
        first_total = dot_tn(features_s[...], first_s[e]) * grad_scale
        held["embed"] = held["embed"] + dot_nt(first_s[e], w_first_ref[e, z.dense :, :])
        found = None
        for k, column in z.columns[e]:
            part = bias_sums[k][column : column + 1, :]
            found = part if found is None else found + part
        keep(3, found)
        line = (e - span[0]) * z.expert_rows
        lines = pl.ds(line, z.expert_rows)
        for shard in range(BLOCKS):
            at = block_of(shard, *places[index])
            begin = line
            for v, count in ((first_total, z.first_rows), (second_total, z.second_rows)):
                for h in range(z.halves):
                    packed_s[index][at, begin : begin + count, :] = v[
                        shard * count : (shard + 1) * count, h * LANES : (h + 1) * LANES
                    ]
                    begin += count
        for side in range(2):
            blocks = pl.ds(side * (BLOCKS // 2), BLOCKS // 2)
            send(packed_s[index].at[blocks, lines, :], piece_refs[index][side].at[:, lines, :])
        yield

    chains = [expert(index, e) for index, span in enumerate(SPANS) for e in range(*span)]
    for _ in range(3):
        next(chains[0])
    for this, then in zip(chains, chains[1:] + [iter([None] * 7)]):
        next(then)
        next(this)
        next(this)
        next(then)
        next(then)
        next(this)
        next(this)
    along, embed = held["along"], held["embed"]
    logit_grad = logit_part(z, weights_s[...], along)
    logit_s[...] = logit_grad
    send(logit_s, logit_ref)
    gate_total = 2.0 * dot_tn(logit_grad, features_s[...])
    embed = 0.5 * embed + dot(logit_grad, gates[:, z.dense :])
    table_total = table_part(z, embed.astype(bf16), spreads, ids_ref, presence_ref)
    small_s[: z.high, :] = table_total.T
    for q in range(z.d_in // LANES):
        line = z.gate_at + q * 16
        small_s[line : line + 16, :] = gate_total[:16, q * LANES : (q + 1) * LANES]
    small_s[z.bias_at :, :] = jnp.zeros_like(small_s[z.bias_at :, :])
    small_s[z.bias_at : z.bias_at + 1, :] = jnp.sum(logit_grad.astype(f32), axis=0, keepdims=True)
    lines = pl.ds((SPANS[-1][1] - SPANS[-1][0]) * z.expert_rows, z.small_rows)
    for shard in range(BLOCKS):
        at = block_of(shard, *places[-1])
        packed_s[-1][at, lines, :] = (
            small_s[shard * z.small_rows : (shard + 1) * z.small_rows, :] * grad_scale
        )
    for side in range(2):
        blocks = pl.ds(side * (BLOCKS // 2), BLOCKS // 2)
        send(packed_s[-1].at[blocks, lines, :], piece_refs[-1][side].at[:, lines, :])
    for copy in sent:
        copy.wait()


def outputs_kernel(z, *refs):
    weights_ref, logit_ref, w_first_ref, gain_ref, bias_ref, gate_task_ref, gate_shared_ref = refs[
        :7
    ]
    normed_ref, first_ref, mixed_ref, dense_ref = refs[7:]
    weights = weights_ref[...]
    mixed = [None] * (z.tasks + 1)
    gates = gate_matrix(z, gate_task_ref, gate_shared_ref)
    dense = None
    for e in range(z.experts):
        expert_out = normed_ref[e].astype(f32) * gain_ref[e : e + 1, :].astype(f32) + bias_ref[
            e : e + 1, :
        ].astype(f32)
        for k, column in z.columns[e]:
            part = weights[:, column : column + 1] * expert_out
            mixed[k] = part if mixed[k] is None else mixed[k] + part
        part = dot_nt(first_ref[e], w_first_ref[e, : z.dense, :])
        dense = part if dense is None else dense + part
    for k in range(z.tasks + 1):
        mixed_ref[k] = mixed[k].astype(bf16)
    dense_ref[...] = 0.5 * dense + dot(logit_ref[...], gates[:, : z.dense])


def unpack_kernel(z, side, device_ref, *refs):
    refs = list(refs)

    def take(count):
        return [refs.pop(0) for _ in range(count)]

    far_refs = take(2 * (len(SPANS) + side))
    if side:
        take(2)
    w_first_ref, w_second_ref = take(2)
    small_outs = take(9 * side)
    here = list(zip(far_refs[::2], far_refs[1::2]))
    w_first_s, w_second_s, out_sems = take(3)
    places = [device_bits(device_ref[0], order) for order in ORDERS]
    core = places[0][0]
    count = BLOCKS // 2
    owner = lax.bitwise_xor(core, side)
    sent = []

    first = HALVED - 1
    for parts, span, (_, own) in zip(here, SPANS, places):
        bit = lax.bitwise_and(lax.shift_right_logical(own, first), 1)
        for e in range(*span):
            for half in range(2):

                @pl.when(bit == half)
                def _():
                    for shard in range(count):
                        part_ref = parts[(shard >> first & 1) ^ half]
                        block = lax.bitwise_and(lax.bitwise_xor(own, shard), count // 2 - 1)
                        line = (e - span[0]) * z.expert_rows
                        for ref, rows in ((w_first_s, z.first_rows), (w_second_s, z.second_rows)):
                            lines = slice(shard * rows, (shard + 1) * rows)
                            for h in range(z.halves):
                                ref[e, lines, h * LANES : (h + 1) * LANES] = part_ref[
                                    block, line : line + rows, :
                                ]
                                line += rows

            for ref, out_ref in ((w_first_s, w_first_ref), (w_second_s, w_second_ref)):
                rows = ref.shape[1]
                lines = pl.ds(pl.multiple_of(owner * rows, rows), rows)
                copy = pltpu.make_async_copy(
                    ref.at[e], out_ref.at[e, lines, :], out_sems.at[len(sent)]
                )
                copy.start()
                sent.append(copy)

    def finish():
        for copy in sent:
            copy.wait()

    if not side:
        finish()
        return
    table_ref, gate_task_ref, gate_task_bias_ref, gate_shared_ref, gate_shared_bias_ref = (
        small_outs[:5]
    )
    sum_refs = small_outs[5:]
    (small_s,) = take(1)

    own = places[-1][1]
    bit = lax.bitwise_and(lax.shift_right_logical(own, first), 1)
    for half, parts in enumerate((here[-1], here[len(SPANS) - 1])):
        start = lax.bitwise_xor(core, half) * (count * z.small_rows)
        for side_bit in range(2):

            @pl.when(bit == side_bit)
            def _():
                for shard in range(count):
                    lines = pl.ds(pl.multiple_of(start + shard * z.small_rows, 8), z.small_rows)
                    part_ref = parts[(shard >> first & 1) ^ side_bit]
                    block = lax.bitwise_and(lax.bitwise_xor(own, shard), count // 2 - 1)
                    small_s[lines, :] = part_ref[block, part_ref.shape[1] - z.small_rows :, :]

    for low in range(z.low):
        table_ref[:, low * z.high : (low + 1) * z.high] = small_s[
            low * z.emb : (low + 1) * z.emb, :
        ]
    for q in range(z.d_in // LANES):
        line = z.gate_at + q * 16
        lanes = slice(q * LANES, (q + 1) * LANES)
        for k in range(z.tasks):
            gate_task_ref[k, :, lanes] = small_s[
                line + k * z.gate : line + (k + 1) * z.gate, :
            ]
        gate_shared_ref[:, lanes] = small_s[line + z.tasks * z.gate : line + z.width, :]
    bias_row = small_s[z.bias_at : z.bias_at + 1, :]
    for k in range(z.tasks):
        gate_task_bias_ref[k : k + 1, :] = bias_row[:, k * z.gate : (k + 1) * z.gate]
    gate_shared_bias_ref[...] = bias_row[:, z.tasks * z.gate : z.width]
    for e in range(z.experts):
        for q in range(4):
            for h in range(z.halves):
                line = z.sums_at + e * z.sum_rows + q * z.halves + h
                sum_refs[q][e : e + 1, h * LANES : (h + 1) * LANES] = small_s[
                    line : line + 1, :
                ]
    finish()


SMEM = pl.BlockSpec(memory_space=pltpu.SMEM)
ANY = pl.BlockSpec(memory_space=pl.ANY)
HBM = pl.BlockSpec(memory_space=pltpu.HBM)


def shape_of(shape, dtype=f32):
    return jax.ShapeDtypeStruct(shape, dtype)


def whole(array):
    return pl.BlockSpec(array.shape, lambda at: (0,) * len(array.shape))


def rows_spec(z, block, shape):
    if shape == (z.fields, z.rows):
        return pl.BlockSpec((z.fields, block), lambda at: (0, at))
    if len(shape) == 2:
        return pl.BlockSpec((block, shape[1]), lambda at: (at, 0))
    return pl.BlockSpec((shape[0], block, shape[2]), lambda at: (0, at, 0))


def run_main(z, grad_scale, device, operands):
    rows = z.rows
    out_shape = []
    for index in range(len(SPANS)):
        out_shape += [shape_of((BLOCKS // 2, z.piece_rows(index), LANES))] * 2
    rows_shape = [
        shape_of((z.experts, rows, z.out), bf16),
        shape_of((z.experts, rows, z.hidden), bf16),
        shape_of((rows, LANES)),
        shape_of((rows, LANES), bf16),
    ]
    out_shape += rows_shape
    scratch = [pltpu.VMEM(v.shape, v.dtype) for v in operands]
    scratch += [pltpu.SemaphoreType.DMA((len(operands),))]
    scratch += [pltpu.SemaphoreType.DMA((4 * z.experts + 4,))]
    scratch += [pltpu.VMEM((rows, z.d_in), bf16)]
    scratch += [pltpu.VMEM(v.shape, v.dtype) for v in rows_shape]
    scratch += [pltpu.VMEM((z.small_rows * BLOCKS, LANES), f32)]
    scratch += [
        pltpu.VMEM((BLOCKS, z.piece_rows(index), LANES), f32) for index in range(len(SPANS))
    ]
    macs = rows * z.experts * 3 * (z.d_in * z.hidden + z.hidden * z.out)
    return pl.pallas_call(
        functools.partial(main_kernel, z, grad_scale),
        in_specs=[SMEM] + [ANY] * len(operands),
        out_specs=[ANY] * len(out_shape),
        out_shape=out_shape,
        scratch_shapes=scratch,
        compiler_params=pltpu.CompilerParams(vmem_limit_bytes=54 * MIB),
        cost_estimate=pl.CostEstimate(
            flops=2 * macs,
            bytes_accessed=20 * MIB,
            transcendentals=rows * z.experts * z.hidden,
        ),
        name="experts",
    )(device, *operands)


def run_outputs(z, weights, logit_grad, w_first, gain, bias, gates, normed, firsts):
    block = z.rows // 4
    out_shape = [shape_of((z.tasks + 1, z.rows, z.out), bf16), shape_of((z.rows, z.dense))]
    return pl.pallas_call(
        functools.partial(outputs_kernel, z),
        grid=(z.rows // block,),
        in_specs=[rows_spec(z, block, v.shape) for v in (weights, logit_grad)]
        + [whole(v) for v in (w_first, gain, bias) + gates]
        + [rows_spec(z, block, v.shape) for v in (normed, firsts)],
        out_specs=[rows_spec(z, block, v.shape) for v in out_shape],
        out_shape=out_shape,
        compiler_params=pltpu.CompilerParams(vmem_limit_bytes=24 * MIB),
        cost_estimate=pl.CostEstimate(
            flops=2 * z.rows * z.experts * z.hidden * z.dense,
            bytes_accessed=11 * MIB,
            transcendentals=0,
        ),
        name="outputs",
    )(weights, logit_grad, w_first, gain, bias, *gates, normed, firsts)


def run_unpack(z, side, device, near, far, earlier):
    out_shape = [
        shape_of((z.experts, z.d_in, z.hidden)),
        shape_of((z.experts, z.hidden, z.out)),
    ]
    halves = [pltpu.VMEM((v.shape[0], v.shape[1] // 2, v.shape[2]), f32) for v in out_shape]
    out_specs = [ANY] * 2
    pieces = list(far if side else near)
    if side:
        pieces.append(near[-1])
    operands = [v for piece in pieces for v in piece]
    aliases = {}
    if side:
        aliases = {1 + len(operands): 0, 2 + len(operands): 1}
        small = [
            shape_of((z.emb, z.vocab)),
            shape_of((z.tasks, z.gate, z.d_in)),
            shape_of((z.tasks, z.gate)),
            shape_of((z.experts, z.d_in)),
            shape_of((1, z.experts)),
        ] + [shape_of((z.experts, z.out))] * 4
        out_shape += small
        out_specs += [pl.BlockSpec(memory_space=pltpu.VMEM)] * len(small)
    vmem = pl.BlockSpec(memory_space=pltpu.VMEM)
    in_specs = [SMEM] + [vmem] * len(operands) + [ANY] * len(earlier)
    scratch = halves
    scratch += [pltpu.SemaphoreType.DMA((2 * z.experts,))]
    if side:
        scratch += [pltpu.VMEM((z.small_rows * BLOCKS, LANES), f32)]
    operands += list(earlier)
    return pl.pallas_call(
        functools.partial(unpack_kernel, z, side),
        in_specs=in_specs,
        out_specs=out_specs,
        out_shape=out_shape,
        scratch_shapes=scratch,
        input_output_aliases=aliases,
        compiler_params=pltpu.CompilerParams(vmem_limit_bytes=24 * MIB),
        cost_estimate=pl.CostEstimate(flops=0, bytes_accessed=4 * MIB, transcendentals=0),
        name="unpack_%d" % side,
    )(device, *operands)


def exchange(value, axis):
    flip = FLIPS[axis]
    count = lax.axis_size("wide") * lax.axis_size("narrow")
    return lax.ppermute(value, BOTH, [(i, i ^ flip) for i in range(count)])


def after(value, other):
    return lax.optimization_barrier((value, other))[0]


def sum_pieces(near, far, outputs):
    count = len(near)
    got = [exchange(v, "c") for v in far]
    sent = None
    for step in range(HALVED):
        for i in range(count):
            found = got[i] if sent is None else after(got[i], sent)
            half = near[i].shape[0] // 2
            low, high = near[i][:half] + found[:half], near[i][half:] + found[half:]
            near[i] = low
            got[i] = exchange(high, ORDERS[i][step])
            sent = high
    for i in range(count):
        near[i] = near[i] + after(got[i], sent)
        got[i] = exchange(near[i], ORDERS[i][HALVED])
        sent = near[i]
    results = outputs(sent)
    sent = results[0]
    early = []
    for step in reversed(range(HALVED)):
        for i in range(count):
            if step < HALVED - 1:
                near[i] = jnp.concatenate([near[i], after(got[i], sent)], axis=0)
            else:
                near[i] = near[i] + after(got[i], sent)
            got[i] = exchange(near[i], ORDERS[i][step])
            sent = near[i]
            if step == 0:
                early.append(exchange(near[i], "c"))
    near_parts, far_parts = [], []
    for i in range(count):
        found = after(got[i], sent)
        sent = found
        near_parts.append((near[i], found))
        far_parts.append((early[i], exchange(found, "c")))
    near, far = near_parts, far_parts
    return near, far, results


def local(
    fits,
    dense_feats,
    sparse_ids,
    presence,
    embed_table,
    w_first,
    b_first,
    w_second,
    b_second,
    ln_gain,
    ln_bias,
    gate_task,
    gate_task_bias,
    gate_shared,
    gate_shared_bias,
    cotangent,
):
    z = Sizes(dense_feats, sparse_ids, embed_table, w_first, w_second, gate_task)
    total_rows = z.rows * lax.axis_size("wide") * lax.axis_size("narrow")
    grad_scale = 1.0 / math.sqrt(total_rows)
    if fits:
        device = lax.axis_index("wide") * lax.axis_size("narrow") + lax.axis_index("narrow")
    else:
        device = 0
    device = jnp.full((1,), device, jnp.int32)
    ids, present = sparse_ids.T, presence.T
    gates = (gate_task.transpose(0, 2, 1), gate_shared.T)
    found = run_main(
        z,
        grad_scale,
        device,
        [
            ids,
            present,
            embed_table.T,
            gates[0],
            gate_task_bias,
            gates[1],
            gate_shared_bias.reshape(1, -1),
            dense_feats,
            w_first,
            b_first,
            w_second,
            b_second,
            ln_gain,
            ln_bias,
            cotangent,
        ],
    )
    near, far = list(found[: 2 * len(SPANS) : 2]), list(found[1 : 2 * len(SPANS) : 2])
    normed, firsts, weights, logit_grad = found[2 * len(SPANS) :]

    def outputs(begin):
        first = weights if begin is None else after(weights, begin)
        return run_outputs(
            z, first, logit_grad, w_first, ln_gain, ln_bias, gates, normed, firsts
        )

    if fits:
        near, far, results = sum_pieces(near, far, outputs)
    else:
        results = outputs(None)
        near, far = lax.psum((near, far), BOTH)
        half = BLOCKS // 4
        near, far = [[(v[:half], v[half:]) for v in side] for side in (near, far)]
    grads = run_unpack(z, 0, device, near, far, ())
    grads = run_unpack(z, 1, device, near, far, grads)
    mixed, dense_grad = results
    w_first_grad, w_second_grad, table_grad = grads[:3]
    gate_task_grad, gate_task_bias_grad, gate_shared_grad, gate_shared_bias_grad = grads[3:7]
    b_first_grad, b_second_grad, gain_grad, bias_grad = grads[7:]
    return (
        mixed,
        dense_grad,
        table_grad.T,
        w_first_grad,
        b_first_grad,
        w_second_grad,
        b_second_grad,
        gain_grad,
        bias_grad,
        gate_task_grad.transpose(0, 2, 1),
        gate_task_bias_grad,
        gate_shared_grad.T,
        gate_shared_bias_grad.reshape(-1),
    )


def solution(mesh):
    fits = (mesh.shape["wide"], mesh.shape["narrow"]) == (8, 4)
    rows = P(BOTH, None)
    middle = P(None, BOTH, None)
    return jax.shard_map(
        functools.partial(local, fits),
        mesh=mesh,
        in_specs=(rows, rows, rows) + (P(),) * 11 + (middle,),
        out_specs=(middle, rows) + (P(),) * 11,
        check_vma=False,
    )
```

```python
import functools
import math

import jax
import jax.numpy as jnp
from jax import lax
from jax.experimental import pallas as pl
from jax.experimental.pallas import tpu as pltpu
from jax.sharding import PartitionSpec as P

f32 = jnp.float32
bf16 = jnp.bfloat16
epsilon = 1e-05
LANES = 128
DEVICES = 32
MIB = 1 << 20
LAG = 2
BOTH = ("wide", "narrow")
SPANS = ((0, 2), (2, 4), (4, 6))
FLIPS = {"c": 1, "x": 2, "y": 4, "1": 8, "2": 16}
ORDERS = ("xy12", "y1x2", "1xy2")
HALVED = 3
BLOCKS = 2 << HALVED


def dot(a, b):
    return lax.dot_general(a, b, (((1,), (0,)), ((), ())), preferred_element_type=f32)


def dot_nt(a, b):
    return lax.dot_general(a, b, (((1,), (1,)), ((), ())), preferred_element_type=f32)


def dot_tn(a, b):
    return lax.dot_general(a, b, (((0,), (0,)), ((), ())), preferred_element_type=f32)


def iota(shape, axis):
    return lax.broadcasted_iota(jnp.int32, shape, axis)


def ones_where(condition):
    return jnp.where(condition, 1.0, 0.0).astype(bf16)


class Sizes:
    def __init__(self, dense, ids, table, w_first, w_second, gate_task):
        self.rows, self.dense = dense.shape
        self.fields = ids.shape[1]
        self.vocab, self.emb = table.shape
        self.experts, self.d_in, self.hidden = w_first.shape
        self.out = w_second.shape[2]
        self.tasks, _, self.gate = gate_task.shape
        self.spec = (self.experts - self.gate) // (self.tasks - 1)
        self.low = LANES // self.emb
        self.high = self.vocab // self.low
        self.columns = gate_columns(self.experts, self.tasks, self.spec)
        self.width = self.tasks * self.gate + self.experts
        self.first_rows = self.d_in // BLOCKS
        self.second_rows = self.hidden // BLOCKS
        self.halves = self.out // LANES
        self.expert_rows = (self.first_rows + self.second_rows) * self.halves
        self.sum_rows = 4 * self.halves
        self.gate_rows = 16 * (self.d_in // LANES)
        self.gate_at = self.high
        self.sums_at = self.gate_at + self.gate_rows
        self.bias_at = self.sums_at + self.experts * self.sum_rows
        self.small_rows = -(-(self.bias_at + 1) // (8 * BLOCKS)) * 8

    def piece_rows(self, index):
        lo, hi = SPANS[index]
        last = index == len(SPANS) - 1
        return (hi - lo) * self.expert_rows + (self.small_rows if last else 0)


def gate_columns(experts, tasks, spec):
    shared = tasks * spec
    gate = spec + experts - shared
    columns = []
    for e in range(experts):
        found = []
        for k in range(tasks):
            if e >= shared:
                found.append((k, k * gate + spec + e - shared))
            elif e // spec == k:
                found.append((k, k * gate + e - k * spec))
        found.append((tasks, tasks * gate + e))
        columns.append(found)
    return columns


def gate_matrix(z, gate_task_ref, gate_shared_ref):
    total = None
    for k in range(z.tasks + 1):
        mat = gate_task_ref[k] if k < z.tasks else gate_shared_ref[...]
        n = mat.shape[0]
        place = ones_where(iota((LANES, n), 0) == iota((LANES, n), 1) + k * z.gate)
        part = dot(place, mat)
        total = part if total is None else total + part
    return total.astype(bf16)


def gate_bias(z, task_ref, shared_ref):
    total = None
    for k in range(z.tasks + 1):
        row = task_ref[k : k + 1, :] if k < z.tasks else shared_ref[...]
        n = row.shape[1]
        place = ones_where(iota((n, LANES), 1) == iota((n, LANES), 0) + k * z.gate)
        part = dot(row, place)
        total = part if total is None else total + part
    return total


def gate_lanes(z, k, shape):
    lane = iota(shape, 1)
    first = k * z.gate
    last = first + (z.gate if k < z.tasks else z.experts)
    return (lane >= first) & (lane < last)


def spread_matrix(z, f):
    a = iota((LANES, LANES), 0)
    b = iota((LANES, LANES), 1)
    return ones_where(b == f * z.emb + lax.rem(a, z.emb))


def table_block(z, table_ref):
    return jnp.concatenate(
        [table_ref[:, low * z.high : (low + 1) * z.high] for low in range(z.low)], axis=0
    )


def split_ids(z, ids_ref, presence_ref):
    ids = ids_ref[...]
    row = jnp.where(presence_ref[...] > 0, lax.bitwise_and(ids, z.high - 1), -1)
    return row, lax.div(ids, z.high)


def turned(v):
    return v.astype(f32).T.astype(jnp.int32)


def lookup_part(z, block, spreads, ids_ref, presence_ref):
    row, low = split_ids(z, ids_ref, presence_ref)
    row, low = turned(row), turned(low)
    lane_high = iota((z.rows, z.high), 1)
    lane_low = lax.div(iota((z.rows, LANES), 1), z.emb)
    total = None
    for f in range(z.fields):
        found = dot_nt(ones_where(row[:, f : f + 1] == lane_high), block)
        kept = jnp.where(low[:, f : f + 1] == lane_low, found, 0.0).astype(bf16)
        part = dot(kept, spreads[f])
        total = part if total is None else total + part
    return total


def softmax_part(z, logits):
    result = None
    for k in range(z.tasks + 1):
        lanes = gate_lanes(z, k, logits.shape)
        top = jnp.max(jnp.where(lanes, logits, -jnp.inf), axis=1, keepdims=True)
        value = jnp.exp(jnp.where(lanes, logits - top, -jnp.inf))
        value = value / jnp.sum(value, axis=1, keepdims=True)
        result = value if result is None else result + value
    return result


def logit_part(z, weights, along):
    product = weights * along
    total = jnp.zeros_like(product)
    for k in range(z.tasks + 1):
        lanes = gate_lanes(z, k, product.shape)
        found = jnp.sum(jnp.where(lanes, product, 0.0), axis=1, keepdims=True)
        total = jnp.where(lanes, found, total)
    return (weights * (along - total)).astype(bf16)


def table_part(z, embed, spreads, ids_ref, presence_ref):
    row, low = split_ids(z, ids_ref, presence_ref)
    low = turned(low)
    line_high = iota((z.high, z.rows), 0)
    lane_low = lax.div(iota((z.rows, LANES), 1), z.emb)
    hots = []
    kept = []
    for f in range(z.fields):
        hots.append(ones_where(row[f : f + 1, :] == line_high))
        wide = dot_nt(embed, spreads[f])
        kept.append(jnp.where(low[:, f : f + 1] == lane_low, wide, 0.0).astype(bf16))
    return dot(jnp.concatenate(hots, axis=1), jnp.concatenate(kept, axis=0))


def device_bits(device, order):
    own = jnp.int32(0)
    for axis in order[:HALVED]:
        own = own * 2 + lax.bitwise_and(lax.div(device, FLIPS[axis]), 1)
    return lax.bitwise_and(device, 1), own


def block_of(shard, core, own):
    count = BLOCKS // 2
    return lax.bitwise_xor(core, shard // count) * count + lax.bitwise_xor(own, shard % count)


def column_matrix(z, k, ref):
    total = None
    row = iota((LANES, z.out), 0)
    for e in range(z.experts):
        for gate, column in z.columns[e]:
            if gate == k:
                part = jnp.where(row == column, ref[e : e + 1, :].astype(f32), 0.0)
                total = part if total is None else total + part
    return total.astype(bf16)


def main_kernel(z, grad_scale, *refs):
    refs = list(refs)

    def take(count):
        return [refs.pop(0) for _ in range(count)]

    (device_ref,) = take(1)
    far_refs = take(15)
    piece_refs = [take(2) for _ in SPANS]
    normed_ref, first_ref, weights_ref, logit_ref = take(4)
    here = take(15)
    sems, out_sems, features_s, normed_s, first_s, weights_s, logit_s, small_s = take(8)
    packed_s = take(len(SPANS))
    copies = [
        pltpu.make_async_copy(a, b, sems.at[i]) for i, (a, b) in enumerate(zip(far_refs, here))
    ]
    for copy in copies:
        copy.start()
    sent = []

    def send(source, target):
        copy = pltpu.make_async_copy(source, target, out_sems.at[len(sent)])
        copy.start()
        sent.append(copy)

    places = [device_bits(device_ref[0], order) for order in ORDERS]
    ids_ref, presence_ref, table_ref, gate_task_ref, gate_task_bias_ref = here[:5]
    gate_shared_ref, gate_shared_bias_ref, dense_ref, w_first_ref, b_first_ref = here[5:10]
    w_second_ref, b_second_ref, gain_ref, bias_ref, cot_ref = here[10:]
    spreads = [spread_matrix(z, f) for f in range(z.fields)]
    for copy in copies[:3]:
        copy.wait()
    looked = lookup_part(z, table_block(z, table_ref), spreads, ids_ref, presence_ref)
    features_s[:, z.dense :] = (0.5 * looked).astype(bf16)
    for copy in copies[3:8]:
        copy.wait()
    features_s[:, : z.dense] = dense_ref[...] * 0.5
    gates = gate_matrix(z, gate_task_ref, gate_shared_ref)
    features = features_s[...]
    logits = 2.0 * dot_nt(features, gates)
    weights = softmax_part(z, logits + gate_bias(z, gate_task_bias_ref, gate_shared_bias_ref))
    weights_s[...] = weights
    send(weights_s, weights_ref)
    for copy in copies[8:]:
        copy.wait()
    lane = iota((z.rows, LANES), 1)
    along = None
    few = weights.astype(bf16)
    bias_sums = []
    for k in range(z.tasks + 1):
        part = dot_nt(cot_ref[k], column_matrix(z, k, bias_ref))
        along = part if along is None else along + part
        bias_sums.append(dot_tn(few, cot_ref[k]))
    held = {"along": along, "embed": jnp.zeros((z.rows, LANES), f32)}
    scale = 1.0 / z.out

    def expert(index, e):
        span = SPANS[index]

        def row(ref):
            return ref[e : e + 1, :].astype(f32)

        def mean(v):
            return jnp.sum(v, axis=1, keepdims=True) * scale

        def keep(q, v):
            for h in range(z.halves):
                line = z.sums_at + e * z.sum_rows + q * z.halves + h
                small_s[line : line + 1, :] = v[:, h * LANES : (h + 1) * LANES]

        def total(v):
            return jnp.sum(v, axis=0, keepdims=True)

        gain = row(gain_ref)
        half = dot(features_s[...], w_first_ref[e]) + 0.5 * row(b_first_ref)
        yield
        turn = jnp.tanh(half)
        up = 1.0 + turn
        smooth = half * up
        hidden = smooth.astype(bf16)
        yield
        second = dot(hidden, w_second_ref[e]) + row(b_second_ref)
        yield
        center = second - mean(second)
        inverse = lax.rsqrt(mean(center * center) + epsilon)
        normed = center * inverse
        normed_s[e] = normed.astype(bf16)
        send(normed_s.at[e], normed_ref.at[e])
        low = normed.astype(bf16)
        low_gain = gain_ref[e : e + 1, :]
        gained = low * low_gain
        upstream = None
        along = held["along"]
        for k, column in z.columns[e]:
            cot = cot_ref[k]
            part = few[:, column : column + 1] * cot
            upstream = part if upstream is None else upstream + part
            found = jnp.sum((cot * gained).astype(f32), axis=1, keepdims=True)
            along = jnp.where(lane == column, along + found, along)
        held["along"] = along
        product = upstream * low
        scaled = upstream * low_gain
        average = jnp.full((z.out, LANES), scale, bf16)
        first_mean = dot(scaled, average).astype(bf16)
        second_mean = dot(product * low_gain, average).astype(bf16)
        first_mean = jnp.concatenate([first_mean] * z.halves, axis=1)
        second_mean = jnp.concatenate([second_mean] * z.halves, axis=1)
        second_grad = inverse.astype(bf16) * (scaled - first_mean - low * second_mean)
        ones = jnp.ones((16, z.rows), bf16)
        keep(1, dot(ones, second_grad)[:1])
        keep(2, dot(ones, product)[:1])
        yield
        hidden_grad = dot_nt(second_grad, w_second_ref[e])
        second_total = dot_tn(hidden, second_grad) * grad_scale
        yield
        first_grad = hidden_grad * (up + smooth * (1.0 - turn))
        keep(0, 0.5 * total(first_grad))
        first_s[e] = first_grad.astype(bf16)
        send(first_s.at[e], first_ref.at[e])
        yield
        first_total = dot_tn(features_s[...], first_s[e]) * grad_scale
        held["embed"] = held["embed"] + dot_nt(first_s[e], w_first_ref[e, z.dense :, :])
        found = None
        for k, column in z.columns[e]:
            part = bias_sums[k][column : column + 1, :]
            found = part if found is None else found + part
        keep(3, found)
        line = (e - span[0]) * z.expert_rows
        lines = pl.ds(line, z.expert_rows)
        for shard in range(BLOCKS):
            at = block_of(shard, *places[index])
            begin = line
            for v, count in ((first_total, z.first_rows), (second_total, z.second_rows)):
                for h in range(z.halves):
                    packed_s[index][at, begin : begin + count, :] = v[
                        shard * count : (shard + 1) * count, h * LANES : (h + 1) * LANES
                    ]
                    begin += count
        for side in range(2):
            blocks = pl.ds(side * (BLOCKS // 2), BLOCKS // 2)
            send(packed_s[index].at[blocks, lines, :], piece_refs[index][side].at[:, lines, :])
        yield

    chains = [expert(index, e) for index, span in enumerate(SPANS) for e in range(*span)]
    for _ in range(3):
        next(chains[0])
    for this, then in zip(chains, chains[1:] + [iter([None] * 7)]):
        next(then)
        next(this)
        next(this)
        next(then)
        next(then)
        next(this)
        next(this)
    along, embed = held["along"], held["embed"]
    logit_grad = logit_part(z, weights_s[...], along)
    logit_s[...] = logit_grad
    send(logit_s, logit_ref)
    gate_total = 2.0 * dot_tn(logit_grad, features_s[...])
    embed = 0.5 * embed + dot(logit_grad, gates[:, z.dense :])
    table_total = table_part(z, embed.astype(bf16), spreads, ids_ref, presence_ref)
    small_s[: z.high, :] = table_total.T
    for q in range(z.d_in // LANES):
        line = z.gate_at + q * 16
        small_s[line : line + 16, :] = gate_total[:16, q * LANES : (q + 1) * LANES]
    small_s[z.bias_at :, :] = jnp.zeros_like(small_s[z.bias_at :, :])
    small_s[z.bias_at : z.bias_at + 1, :] = jnp.sum(logit_grad.astype(f32), axis=0, keepdims=True)
    lines = pl.ds((SPANS[-1][1] - SPANS[-1][0]) * z.expert_rows, z.small_rows)
    for shard in range(BLOCKS):
        at = block_of(shard, *places[-1])
        packed_s[-1][at, lines, :] = (
            small_s[shard * z.small_rows : (shard + 1) * z.small_rows, :] * grad_scale
        )
    for side in range(2):
        blocks = pl.ds(side * (BLOCKS // 2), BLOCKS // 2)
        send(packed_s[-1].at[blocks, lines, :], piece_refs[-1][side].at[:, lines, :])
    for copy in sent:
        copy.wait()


def outputs_kernel(z, *refs):
    weights_ref, logit_ref, w_first_ref, gain_ref, bias_ref, gate_task_ref, gate_shared_ref = refs[
        :7
    ]
    normed_ref, first_ref, mixed_ref, dense_ref = refs[7:]
    weights = weights_ref[...]
    mixed = [None] * (z.tasks + 1)
    gates = gate_matrix(z, gate_task_ref, gate_shared_ref)
    dense = None
    for e in range(z.experts):
        expert_out = normed_ref[e].astype(f32) * gain_ref[e : e + 1, :].astype(f32) + bias_ref[
            e : e + 1, :
        ].astype(f32)
        for k, column in z.columns[e]:
            part = weights[:, column : column + 1] * expert_out
            mixed[k] = part if mixed[k] is None else mixed[k] + part
        part = dot_nt(first_ref[e], w_first_ref[e, : z.dense, :])
        dense = part if dense is None else dense + part
    for k in range(z.tasks + 1):
        mixed_ref[k] = mixed[k].astype(bf16)
    dense_ref[...] = 0.5 * dense + dot(logit_ref[...], gates[:, : z.dense])


def unpack_kernel(z, side, device_ref, *refs):
    refs = list(refs)

    def take(count):
        return [refs.pop(0) for _ in range(count)]

    far_refs = take(2 * (len(SPANS) + side))
    if side:
        take(2)
    w_first_ref, w_second_ref = take(2)
    small_outs = take(9 * side)
    here = list(zip(far_refs[::2], far_refs[1::2]))
    w_first_s, w_second_s, out_sems = take(3)
    places = [device_bits(device_ref[0], order) for order in ORDERS]
    core = places[0][0]
    count = BLOCKS // 2
    owner = lax.bitwise_xor(core, side)
    sent = []

    first = HALVED - 1
    for parts, span, (_, own) in zip(here, SPANS, places):
        bit = lax.bitwise_and(lax.shift_right_logical(own, first), 1)
        for e in range(*span):
            for half in range(2):

                @pl.when(bit == half)
                def _():
                    for shard in range(count):
                        part_ref = parts[(shard >> first & 1) ^ half]
                        block = lax.bitwise_and(lax.bitwise_xor(own, shard), count // 2 - 1)
                        line = (e - span[0]) * z.expert_rows
                        for ref, rows in ((w_first_s, z.first_rows), (w_second_s, z.second_rows)):
                            lines = slice(shard * rows, (shard + 1) * rows)
                            for h in range(z.halves):
                                ref[e, lines, h * LANES : (h + 1) * LANES] = part_ref[
                                    block, line : line + rows, :
                                ]
                                line += rows

            for ref, out_ref in ((w_first_s, w_first_ref), (w_second_s, w_second_ref)):
                rows = ref.shape[1]
                lines = pl.ds(pl.multiple_of(owner * rows, rows), rows)
                copy = pltpu.make_async_copy(
                    ref.at[e], out_ref.at[e, lines, :], out_sems.at[len(sent)]
                )
                copy.start()
                sent.append(copy)

    def finish():
        for copy in sent:
            copy.wait()

    if not side:
        finish()
        return
    table_ref, gate_task_ref, gate_task_bias_ref, gate_shared_ref, gate_shared_bias_ref = (
        small_outs[:5]
    )
    sum_refs = small_outs[5:]
    (small_s,) = take(1)

    own = places[-1][1]
    bit = lax.bitwise_and(lax.shift_right_logical(own, first), 1)
    for half, parts in enumerate((here[-1], here[len(SPANS) - 1])):
        start = lax.bitwise_xor(core, half) * (count * z.small_rows)
        for side_bit in range(2):

            @pl.when(bit == side_bit)
            def _():
                for shard in range(count):
                    lines = pl.ds(pl.multiple_of(start + shard * z.small_rows, 8), z.small_rows)
                    part_ref = parts[(shard >> first & 1) ^ side_bit]
                    block = lax.bitwise_and(lax.bitwise_xor(own, shard), count // 2 - 1)
                    small_s[lines, :] = part_ref[block, part_ref.shape[1] - z.small_rows :, :]

    for low in range(z.low):
        table_ref[:, low * z.high : (low + 1) * z.high] = small_s[
            low * z.emb : (low + 1) * z.emb, :
        ]
    for q in range(z.d_in // LANES):
        line = z.gate_at + q * 16
        lanes = slice(q * LANES, (q + 1) * LANES)
        for k in range(z.tasks):
            gate_task_ref[k, :, lanes] = small_s[
                line + k * z.gate : line + (k + 1) * z.gate, :
            ]
        gate_shared_ref[:, lanes] = small_s[line + z.tasks * z.gate : line + z.width, :]
    bias_row = small_s[z.bias_at : z.bias_at + 1, :]
    for k in range(z.tasks):
        gate_task_bias_ref[k : k + 1, :] = bias_row[:, k * z.gate : (k + 1) * z.gate]
    gate_shared_bias_ref[...] = bias_row[:, z.tasks * z.gate : z.width]
    for e in range(z.experts):
        for q in range(4):
            for h in range(z.halves):
                line = z.sums_at + e * z.sum_rows + q * z.halves + h
                sum_refs[q][e : e + 1, h * LANES : (h + 1) * LANES] = small_s[
                    line : line + 1, :
                ]
    finish()


SMEM = pl.BlockSpec(memory_space=pltpu.SMEM)
ANY = pl.BlockSpec(memory_space=pl.ANY)
HBM = pl.BlockSpec(memory_space=pltpu.HBM)


def shape_of(shape, dtype=f32):
    return jax.ShapeDtypeStruct(shape, dtype)


def whole(array):
    return pl.BlockSpec(array.shape, lambda at: (0,) * len(array.shape))


def rows_spec(z, block, shape):
    if shape == (z.fields, z.rows):
        return pl.BlockSpec((z.fields, block), lambda at: (0, at))
    if len(shape) == 2:
        return pl.BlockSpec((block, shape[1]), lambda at: (at, 0))
    return pl.BlockSpec((shape[0], block, shape[2]), lambda at: (0, at, 0))


def run_main(z, grad_scale, device, operands):
    rows = z.rows
    out_shape = []
    for index in range(len(SPANS)):
        out_shape += [shape_of((BLOCKS // 2, z.piece_rows(index), LANES))] * 2
    rows_shape = [
        shape_of((z.experts, rows, z.out), bf16),
        shape_of((z.experts, rows, z.hidden), bf16),
        shape_of((rows, LANES)),
        shape_of((rows, LANES), bf16),
    ]
    out_shape += rows_shape
    scratch = [pltpu.VMEM(v.shape, v.dtype) for v in operands]
    scratch += [pltpu.SemaphoreType.DMA((len(operands),))]
    scratch += [pltpu.SemaphoreType.DMA((4 * z.experts + 4,))]
    scratch += [pltpu.VMEM((rows, z.d_in), bf16)]
    scratch += [pltpu.VMEM(v.shape, v.dtype) for v in rows_shape]
    scratch += [pltpu.VMEM((z.small_rows * BLOCKS, LANES), f32)]
    scratch += [
        pltpu.VMEM((BLOCKS, z.piece_rows(index), LANES), f32) for index in range(len(SPANS))
    ]
    macs = rows * z.experts * 3 * (z.d_in * z.hidden + z.hidden * z.out)
    return pl.pallas_call(
        functools.partial(main_kernel, z, grad_scale),
        in_specs=[SMEM] + [ANY] * len(operands),
        out_specs=[ANY] * len(out_shape),
        out_shape=out_shape,
        scratch_shapes=scratch,
        compiler_params=pltpu.CompilerParams(vmem_limit_bytes=54 * MIB),
        cost_estimate=pl.CostEstimate(
            flops=2 * macs,
            bytes_accessed=20 * MIB,
            transcendentals=rows * z.experts * z.hidden,
        ),
        name="experts",
    )(device, *operands)


def run_outputs(z, weights, logit_grad, w_first, gain, bias, gates, normed, firsts):
    block = z.rows // 2
    out_shape = [shape_of((z.tasks + 1, z.rows, z.out), bf16), shape_of((z.rows, z.dense))]
    return pl.pallas_call(
        functools.partial(outputs_kernel, z),
        grid=(z.rows // block,),
        in_specs=[rows_spec(z, block, v.shape) for v in (weights, logit_grad)]
        + [whole(v) for v in (w_first, gain, bias) + gates]
        + [rows_spec(z, block, v.shape) for v in (normed, firsts)],
        out_specs=[rows_spec(z, block, v.shape) for v in out_shape],
        out_shape=out_shape,
        compiler_params=pltpu.CompilerParams(vmem_limit_bytes=24 * MIB),
        cost_estimate=pl.CostEstimate(
            flops=2 * z.rows * z.experts * z.hidden * z.dense,
            bytes_accessed=11 * MIB,
            transcendentals=0,
        ),
        name="outputs",
    )(weights, logit_grad, w_first, gain, bias, *gates, normed, firsts)


def run_unpack(z, side, device, near, far, earlier):
    out_shape = [
        shape_of((z.experts, z.d_in, z.hidden)),
        shape_of((z.experts, z.hidden, z.out)),
    ]
    halves = [pltpu.VMEM((v.shape[0], v.shape[1] // 2, v.shape[2]), f32) for v in out_shape]
    out_specs = [ANY] * 2
    pieces = list(far if side else near)
    if side:
        pieces.append(near[-1])
    operands = [v for piece in pieces for v in piece]
    aliases = {}
    if side:
        aliases = {1 + len(operands): 0, 2 + len(operands): 1}
        small = [
            shape_of((z.emb, z.vocab)),
            shape_of((z.tasks, z.gate, z.d_in)),
            shape_of((z.tasks, z.gate)),
            shape_of((z.experts, z.d_in)),
            shape_of((1, z.experts)),
        ] + [shape_of((z.experts, z.out))] * 4
        out_shape += small
        out_specs += [pl.BlockSpec(memory_space=pltpu.VMEM)] * len(small)
    vmem = pl.BlockSpec(memory_space=pltpu.VMEM)
    in_specs = [SMEM] + [vmem] * len(operands) + [ANY] * len(earlier)
    scratch = halves
    scratch += [pltpu.SemaphoreType.DMA((2 * z.experts,))]
    if side:
        scratch += [pltpu.VMEM((z.small_rows * BLOCKS, LANES), f32)]
    operands += list(earlier)
    return pl.pallas_call(
        functools.partial(unpack_kernel, z, side),
        in_specs=in_specs,
        out_specs=out_specs,
        out_shape=out_shape,
        scratch_shapes=scratch,
        input_output_aliases=aliases,
        compiler_params=pltpu.CompilerParams(vmem_limit_bytes=24 * MIB),
        cost_estimate=pl.CostEstimate(flops=0, bytes_accessed=4 * MIB, transcendentals=0),
        name="unpack_%d" % side,
    )(device, *operands)


def exchange(value, axis):
    flip = FLIPS[axis]
    count = lax.axis_size("wide") * lax.axis_size("narrow")
    return lax.ppermute(value, BOTH, [(i, i ^ flip) for i in range(count)])


def after(value, other):
    return lax.optimization_barrier((value, other))[0]


def sum_pieces(near, far, outputs):
    count = len(near)
    got = [exchange(v, "c") for v in far]
    sent = None
    for step in range(HALVED):
        for i in range(count):
            found = got[i] if sent is None else after(got[i], sent)
            half = near[i].shape[0] // 2
            low, high = near[i][:half] + found[:half], near[i][half:] + found[half:]
            near[i] = low
            got[i] = exchange(high, ORDERS[i][step])
            sent = high
    for i in range(count):
        near[i] = near[i] + after(got[i], sent)
        got[i] = exchange(near[i], ORDERS[i][HALVED])
        sent = near[i]
    results = outputs(sent)
    sent = results[0]
    early = []
    for step in reversed(range(HALVED)):
        for i in range(count):
            if step < HALVED - 1:
                near[i] = jnp.concatenate([near[i], after(got[i], sent)], axis=0)
            else:
                near[i] = near[i] + after(got[i], sent)
            got[i] = exchange(near[i], ORDERS[i][step])
            sent = near[i]
            if step == 0:
                early.append(exchange(near[i], "c"))
    near_parts, far_parts = [], []
    for i in range(count):
        found = after(got[i], sent)
        sent = found
        near_parts.append((near[i], found))
        far_parts.append((early[i], exchange(found, "c")))
    near, far = near_parts, far_parts
    return near, far, results


def local(
    fits,
    dense_feats,
    sparse_ids,
    presence,
    embed_table,
    w_first,
    b_first,
    w_second,
    b_second,
    ln_gain,
    ln_bias,
    gate_task,
    gate_task_bias,
    gate_shared,
    gate_shared_bias,
    cotangent,
):
    z = Sizes(dense_feats, sparse_ids, embed_table, w_first, w_second, gate_task)
    total_rows = z.rows * lax.axis_size("wide") * lax.axis_size("narrow")
    grad_scale = 1.0 / math.sqrt(total_rows)
    if fits:
        device = lax.axis_index("wide") * lax.axis_size("narrow") + lax.axis_index("narrow")
    else:
        device = 0
    device = jnp.full((1,), device, jnp.int32)
    ids, present = sparse_ids.T, presence.T
    gates = (gate_task.transpose(0, 2, 1), gate_shared.T)
    found = run_main(
        z,
        grad_scale,
        device,
        [
            ids,
            present,
            embed_table.T,
            gates[0],
            gate_task_bias,
            gates[1],
            gate_shared_bias.reshape(1, -1),
            dense_feats,
            w_first,
            b_first,
            w_second,
            b_second,
            ln_gain,
            ln_bias,
            cotangent,
        ],
    )
    near, far = list(found[: 2 * len(SPANS) : 2]), list(found[1 : 2 * len(SPANS) : 2])
    normed, firsts, weights, logit_grad = found[2 * len(SPANS) :]

    def outputs(begin):
        first = weights if begin is None else after(weights, begin)
        return run_outputs(
            z, first, logit_grad, w_first, ln_gain, ln_bias, gates, normed, firsts
        )

    if fits:
        near, far, results = sum_pieces(near, far, outputs)
    else:
        results = outputs(None)
        near, far = lax.psum((near, far), BOTH)
        half = BLOCKS // 4
        near, far = [[(v[:half], v[half:]) for v in side] for side in (near, far)]
    grads = run_unpack(z, 0, device, near, far, ())
    grads = run_unpack(z, 1, device, near, far, grads)
    mixed, dense_grad = results
    w_first_grad, w_second_grad, table_grad = grads[:3]
    gate_task_grad, gate_task_bias_grad, gate_shared_grad, gate_shared_bias_grad = grads[3:7]
    b_first_grad, b_second_grad, gain_grad, bias_grad = grads[7:]
    return (
        mixed,
        dense_grad,
        table_grad.T,
        w_first_grad,
        b_first_grad,
        w_second_grad,
        b_second_grad,
        gain_grad,
        bias_grad,
        gate_task_grad.transpose(0, 2, 1),
        gate_task_bias_grad,
        gate_shared_grad.T,
        gate_shared_bias_grad.reshape(-1),
    )


def solution(mesh):
    fits = (mesh.shape["wide"], mesh.shape["narrow"]) == (8, 4)
    rows = P(BOTH, None)
    middle = P(None, BOTH, None)
    return jax.shard_map(
        functools.partial(local, fits),
        mesh=mesh,
        in_specs=(rows, rows, rows) + (P(),) * 11 + (middle,),
        out_specs=(middle, rows) + (P(),) * 11,
        check_vma=False,
    )
```
